32 devices in a mesh: group: 2 (over y), dp: 4 (over z), expert: 4 (over x, core).
Axes of the slice: x: 2, y: 2, z: 4, core: 2. Of those that a mesh axis runs over, the one named last changes fastest.
Arguments:
- tokens: bfloat16 [1024, 6144], P(('group', 'dp'), 'expert'), parts along dimension 0, may hold values from -6 to 6
- cotangent: bfloat16 [1024, 6144], P(('group', 'dp'), 'expert'), parts along dimension 0, may hold values from -6 to 6
- expert_ids: int32 [1024, 2], P(('group', 'dp')), parts along dimension 0, may hold values from 0 to 7, as said below
- quantized: int32 [1024, 2], P(('group', 'dp')), parts along dimension 0, may hold values from 1 to 65535
- weight_in: bfloat16 [2, 8192, 6144], P(None, 'dp', 'expert'), may hold values from -0.078125 to 0.078125
- weight_out: bfloat16 [8192, 6144], P('dp', 'expert'), may hold values from -0.0625 to 0.0625
Outputs:
- input_grad: bfloat16 [1024, 6144], P(('group', 'dp'), 'expert'), parts along dimension 0
- weight_grad: bfloat16 [1024, 2], P(('group', 'dp')), parts along dimension 0
- grad_weight_in: float32 [4, 8192, 6144], P('group', 'dp', 'expert'), parts along dimension 0
- grad_weight_out: float32 [16384, 6144], P(('group', 'dp'), 'expert'), parts along dimension 0
The draws below stay inside these ranges and needn't reach their ends.
There are 2 independent parts, one for each index of `group`. The reference program is written for one: setup_inputs(seed, part) draws one part's arguments, and reference() takes and returns one part's arrays. A program takes and returns all parts, laid end to end along the dimension named above; an argument that names none is the same for every part. Nothing has to cross between parts.
Inputs may be any that keep to these rules, and one draw needn't show every extreme that they name: `expert_ids`: each row names 2 different experts. Among the 128 rows of one index of dp at most 32 name expert 0, and for some index exactly 32 do.
All inputs are finite; a program needn't handle non-finite values.
Results may differ from the reference program's by a relative error of at most 0.008.
Values may be sent and summed in bfloat16 or wider, within the bound.
No kernel may reach another device: no remote copies, remote signals or barrier semaphores. Data moves between devices by JAX's collectives and lax.ppermute only.
A program may use at most 128 MiB of HBM per device.

```python
import jax
import jax.numpy as jnp

D = 6144
EXPERTS = 8
TOP = 2
HID = 8192
TOK_DEV = 128
CAP = 32
TOKENS = 512


def draw_expert_ids(key, part):
    key = jax.random.fold_in(key, 11)
    blocks = TOKENS // TOK_DEV
    keys = jax.random.split(key, 7)
    counts = jax.random.randint(keys[0], (blocks,), 5 * CAP // 8, CAP + 1)
    full_block = jax.random.randint(keys[1], (), 0, blocks)
    counts = jnp.where(jnp.arange(blocks, dtype=jnp.int32) == full_block, CAP, counts)
    scores = jax.random.randint(keys[2], (blocks, TOK_DEV), 0, 2 ** 20) * TOK_DEV + jnp.arange(TOK_DEV, dtype=jnp.int32)[None, :]
    order = jnp.argsort(scores, axis=1, stable=True)
    ranks = jnp.argsort(order, axis=1, stable=True).astype(jnp.int32)
    to_zero = ranks < counts[:, None]
    first = jnp.where(to_zero, 0, jax.random.randint(keys[3], (blocks, TOK_DEV), 1, EXPERTS))
    after_zero = jax.random.randint(keys[4], (blocks, TOK_DEV), 1, EXPERTS)
    others = jax.random.randint(keys[5], (blocks, TOK_DEV), 1, EXPERTS - 1)
    second = jnp.where(first == 0, after_zero, others + (others >= first).astype(jnp.int32))
    swapped = jax.random.randint(keys[6], (blocks, TOK_DEV), 0, 2) > 0
    column_a = jnp.where(swapped, second, first)
    column_b = jnp.where(swapped, first, second)
    return jnp.stack([column_a, column_b], axis=2).reshape(TOKENS, 2).astype(jnp.int32)


def place_ends(drawn, key, low, high):
    extent = drawn.shape
    spot = [jax.random.randint(jax.random.fold_in(key, axis), (), 0, extent[axis]) for axis in range(len(extent))]
    drawn = drawn.at[tuple(spot)].set(low)
    longest = extent.index(max(extent))
    spot[longest] = (spot[longest] + 1) % extent[longest]
    return drawn.at[tuple(spot)].set(high)


def block_scale(key, extent, cuts, low, high):
    gain = 1.0
    for dim, shards_of in cuts:
        steps = jax.random.uniform(jax.random.fold_in(jax.random.fold_in(key, 6), dim), (shards_of,), jnp.float32, low / len(cuts), high / len(cuts))
        gain = gain * jnp.repeat(jnp.exp(steps), extent[dim] // shards_of).reshape((-1,) + (1,) * (len(extent) - 1 - dim))
    return gain


def noise(key, dims, scale, most, cuts=(), kind=jnp.bfloat16):
    values = jax.random.normal(key, dims, jnp.float32) * scale
    if len(cuts) > 0:
        values = block_scale(key, dims, cuts, -0.22, 0.18) * values
    return jnp.clip(values, min=-most, max=most).astype(kind)


def setup_inputs(seed: int = 0, part: int = 0) -> dict:
    key_of = jax.random.split(jax.random.key(seed), 7)
    part_keys = jax.random.split(jax.random.fold_in(key_of[6], part), 7)
    tokens = noise(part_keys[0], (TOKENS, D), 1.0, 6.0, ((0, 4), (1, 4)))
    cotangent = noise(part_keys[1], (TOKENS, D), 1.0, 6.0, ((0, 4), (1, 4)))
    expert_ids = draw_expert_ids(jax.random.fold_in(jax.random.fold_in(key_of[6], part), 71), part)
    quantized = place_ends(jax.random.randint(part_keys[3], (TOKENS, TOP), 1, 65536), jax.random.fold_in(part_keys[3], 1), 1, 65535).astype(jnp.int32)
    weight_in = noise(key_of[4], (2, HID, D), D ** -0.5, 0.078125, ((1, 4), (2, 4)))
    weight_out = noise(key_of[5], (HID, D), HID ** -0.5, 0.0625, ((0, 4), (1, 4)))
    return dict(tokens=tokens, cotangent=cotangent, expert_ids=expert_ids, quantized=quantized, weight_in=weight_in, weight_out=weight_out)


def routing_weights(quantized):
    scaled = quantized.astype(jnp.float32)
    return (scaled / jnp.sum(scaled, axis=1, keepdims=True)).astype(jnp.bfloat16)


def reference(tokens, cotangent, expert_ids, quantized, weight_in, weight_out):
    routing = routing_weights(quantized)
    chosen = expert_ids == 0
    rate = jnp.sum(jnp.where(chosen, routing.astype(jnp.float32), jnp.zeros((), jnp.float32)), axis=1)
    blocks = TOKENS // TOK_DEV
    routed = jnp.any(chosen, axis=1).astype(jnp.int32).reshape(blocks, TOK_DEV)
    order = jnp.argsort(1 - routed, axis=1, stable=True)[:, :CAP].astype(jnp.int32)
    picks = (order + (jnp.arange(blocks, dtype=jnp.int32) * TOK_DEV)[:, None]).reshape(-1).astype(jnp.int32)
    valid = jnp.take_along_axis(routed, order, axis=1).reshape(-1).astype(jnp.float32)
    tokens_f = tokens[picks].astype(jnp.float32)
    cot_f = cotangent[picks].astype(jnp.float32)
    rate_rows = rate[picks]
    projected = jnp.einsum("td,khd->tkh", tokens_f, weight_in.astype(jnp.float32))
    gate_pre = projected[:, 0]
    up_pre = projected[:, 1]
    sigmoid_gate = jax.nn.sigmoid(gate_pre)
    hidden = (gate_pre * sigmoid_gate * up_pre).astype(jnp.bfloat16)
    back_hidden = jnp.einsum("td,hd->th", cot_f, weight_out.astype(jnp.float32))
    route_sum = jnp.sum(hidden.astype(jnp.float32) * back_hidden, axis=1)
    route_all = jnp.zeros((TOKENS,), jnp.float32).at[picks].add(route_sum * valid)
    weight_grad = jnp.where(chosen, route_all[:, None], jnp.zeros((), jnp.float32)).astype(jnp.bfloat16)
    hidden_grad = rate_rows[:, None] * back_hidden
    gate_grad = hidden_grad * up_pre * sigmoid_gate * (1.0 + gate_pre * (1.0 - sigmoid_gate))
    up_grad = hidden_grad * gate_pre * sigmoid_gate
    pre_grad = jnp.stack([gate_grad, up_grad], axis=1).astype(jnp.bfloat16)
    row_grad = jnp.einsum("tkh,khd->td", pre_grad.astype(jnp.float32), weight_in.astype(jnp.float32))
    input_grad = jnp.zeros((TOKENS, D), jnp.float32).at[picks].add(row_grad * valid[:, None]).astype(jnp.bfloat16)
    out_grad = (rate_rows[:, None] * cot_f).astype(jnp.bfloat16)
    grad_weight_in = jnp.einsum("tkh,td->khd", pre_grad.astype(jnp.float32), tokens_f)
    grad_weight_out = jnp.einsum("th,td->hd", hidden.astype(jnp.float32), out_grad.astype(jnp.float32))
    return (input_grad, weight_grad, grad_weight_in, grad_weight_out)
```

```python
import functools

import jax
import jax.numpy as jnp
from jax import lax
from jax.experimental import pallas as pl
from jax.experimental.pallas import tpu as pltpu
from jax.sharding import PartitionSpec as P

F32 = jnp.float32
BF16 = jnp.bfloat16
VMEM = pl.BlockSpec(memory_space=pltpu.VMEM)
SMEM = pl.BlockSpec(memory_space=pltpu.SMEM)
ANY = pl.BlockSpec(memory_space=pl.ANY)
LANES = 128
MIB = 2**20

NT = (((1,), (1,)), ((), ()))
TN = (((0,), (0,)), ((), ()))


def params(mib):
    return pltpu.CompilerParams(vmem_limit_bytes=mib * MIB)


def cost(flops, nbytes):
    return pl.CostEstimate(flops=int(flops), bytes_accessed=int(nbytes), transcendentals=0)


def slot_selector(ids, capacity):
    tok_rows = ids.shape[0]
    routed = jnp.logical_or(ids[:, 0:1] == 0, ids[:, 1:2] == 0)
    row = lax.broadcasted_iota(jnp.int32, (tok_rows, tok_rows), 0)
    col = lax.broadcasted_iota(jnp.int32, (tok_rows, tok_rows), 1)
    before = jnp.where(col < row, 1.0, 0.0).astype(BF16)
    flags = jnp.broadcast_to(jnp.where(routed, 1.0, 0.0), (tok_rows, capacity))
    position = jnp.dot(before, flags.astype(BF16), preferred_element_type=F32)
    slot = lax.broadcasted_iota(jnp.int32, (tok_rows, capacity), 1).astype(F32)
    return jnp.where(position == slot, flags, 0.0)


def select_kernel(tok_ref, cot_ref, ids_ref, quant_ref, in_ref, grad_ref):
    capacity, width = in_ref.shape
    ids = ids_ref[...]
    picker = slot_selector(ids, capacity).astype(BF16)
    scaled = quant_ref[...].astype(F32)
    total = scaled[:, 0:1] + scaled[:, 1:2]
    routing = (scaled / total).astype(BF16).astype(F32)
    weight = jnp.where(ids == 0, routing, 0.0)
    rate = jnp.broadcast_to(weight[:, 0:1] + weight[:, 1:2], (ids.shape[0], LANES)).astype(BF16)
    in_ref[...] = lax.dot_general(picker, tok_ref[...], TN, preferred_element_type=F32).astype(BF16)
    grad_ref[:, :width] = lax.dot_general(
        picker, cot_ref[...], TN, preferred_element_type=F32
    ).astype(BF16)
    grad_ref[:, width:] = lax.dot_general(picker, rate, TN, preferred_element_type=F32).astype(BF16)


def select(tokens, cotangent, expert_ids, quantized):
    capacity, width = tokens.shape[0] // 4, tokens.shape[1]
    return pl.pallas_call(
        select_kernel,
        in_specs=[VMEM] * 4,
        out_specs=[VMEM] * 2,
        out_shape=[
            jax.ShapeDtypeStruct((capacity, width), BF16),
            jax.ShapeDtypeStruct((capacity, width + LANES), BF16),
        ],
        compiler_params=params(8),
        name="select",
    )(tokens, cotangent, expert_ids, quantized)


def project_kernel(nblocks, width, first_ref, *refs):
    blocks, (w_ref, out_ref) = refs[:nblocks], refs[nblocks:]
    kinds = w_ref.shape[0]
    half = out_ref.shape[1] // kinds
    rows = jnp.concatenate([b[:, :width] for b in blocks], axis=0)
    start = pl.multiple_of(first_ref[0], half)
    step = min(half, 512)
    for kind in range(kinds):
        for j in range(0, half, step):
            out_ref[:, kind * half + j : kind * half + j + step] = lax.dot_general(
                rows, w_ref[kind, pl.ds(start + j, step), :], NT, preferred_element_type=F32
            ).astype(out_ref.dtype)


def project(blocks, weight, first, out_type):
    kinds, hidden, width = weight.shape
    half = hidden // 2
    rows = sum(b.shape[0] for b in blocks)
    return pl.pallas_call(
        functools.partial(project_kernel, len(blocks), width),
        in_specs=[SMEM] + [VMEM] * (len(blocks) + 1),
        out_specs=VMEM,
        out_shape=jax.ShapeDtypeStruct((rows, kinds * half), out_type),
        compiler_params=params(24),
        cost_estimate=cost(2 * rows * kinds * half * width, 2 * kinds * half * width),
        name="project",
    )(first, *blocks, weight)


def gated(sums):
    half = sums.shape[1] // 2
    gate, up = sums[:, :half], sums[:, half:]
    return gate, up, jax.nn.sigmoid(gate)


def hidden_kernel(ngroups, nparts, *refs):
    out_ref = refs[-1]
    parts = refs[:-1]
    at = 0
    for g in range(ngroups):
        group = parts[g * nparts : (g + 1) * nparts]
        sums = sum(p[...].astype(F32) for p in group)
        gate, up, s = gated(sums)
        rows = gate.shape[0]
        out_ref[at : at + rows, :] = (gate * s * up).astype(BF16)
        at += rows


def hidden_units(groups):
    half = groups[0][0].shape[1] // 2
    rows = sum(g[0].shape[0] for g in groups)
    flat = [p for g in groups for p in g]
    return pl.pallas_call(
        functools.partial(hidden_kernel, len(groups), len(groups[0])),
        in_specs=[VMEM] * len(flat),
        out_specs=VMEM,
        out_shape=jax.ShapeDtypeStruct((rows, half), BF16),
        compiler_params=params(16),
        name="hidden",
    )(*flat)


def pre_kernel(ngroups, nparts, nblocks, width, *refs):
    gu = refs[: ngroups * nparts]
    back_parts = refs[ngroups * nparts : ngroups * nparts + nparts]
    blocks = refs[ngroups * nparts + nparts : -1]
    out_ref = refs[-1]
    half = back_parts[0].shape[1]
    at = 0
    for g in range(ngroups):
        group = gu[g * nparts : (g + 1) * nparts]
        sums = sum(p[...].astype(F32) for p in group)
        gate, up, s = gated(sums)
        rows = gate.shape[0]
        back = sum(p[at : at + rows, :].astype(F32) for p in back_parts)
        cap = blocks[0].shape[0]
        rate = jnp.concatenate(
            [
                blocks[i][:, width : width + 1].astype(F32)
                for i in range(at // cap, (at + rows) // cap)
            ],
            axis=0,
        )
        hidden = (gate * s * up).astype(BF16).astype(F32)
        route = jnp.sum(hidden * back, axis=1, keepdims=True)
        grad = rate * back
        gate_grad = grad * up * s * (1.0 + gate * (1.0 - s))
        up_grad = grad * gate * s
        out_ref[at : at + rows, :half] = gate_grad.astype(BF16)
        out_ref[at : at + rows, half : 2 * half] = up_grad.astype(BF16)
        out_ref[at : at + rows, 2 * half :] = high_low(route)
        at += rows


def high_low(value):
    high = value.astype(BF16).astype(F32)
    low = value - high
    lane = lax.broadcasted_iota(jnp.int32, (value.shape[0], LANES), 1)
    return jnp.where(lane == 0, high, jnp.where(lane == 1, low, 0.0)).astype(BF16)


def pre_grads(groups, back_parts, blocks, width):
    half = back_parts[0].shape[1]
    rows = back_parts[0].shape[0]
    flat = [p for g in groups for p in g]
    return pl.pallas_call(
        functools.partial(pre_kernel, len(groups), len(groups[0]), len(blocks), width),
        in_specs=[VMEM] * (len(flat) + len(back_parts) + len(blocks)),
        out_specs=VMEM,
        out_shape=jax.ShapeDtypeStruct((rows, 2 * half + LANES), BF16),
        compiler_params=params(16),
        name="pre",
    )(*flat, *back_parts, *blocks)


def row_own_kernel(first_ref, pre_ref, w_ref, out_ref):
    half = (pre_ref.shape[1] - LANES) // 2
    start = pl.multiple_of(first_ref[0], half)
    out_ref[...] = jnp.dot(
        pre_ref[:, :half], w_ref[0, pl.ds(start, half), :], preferred_element_type=F32
    ) + jnp.dot(
        pre_ref[:, half : 2 * half], w_ref[1, pl.ds(start, half), :], preferred_element_type=F32
    )


def row_own(pre, weight, first):
    rows, width = pre.shape[0], weight.shape[2]
    return pl.pallas_call(
        row_own_kernel,
        in_specs=[SMEM, VMEM, VMEM],
        out_specs=VMEM,
        out_shape=jax.ShapeDtypeStruct((rows, width), F32),
        compiler_params=params(24),
        cost_estimate=cost(2 * rows * weight.shape[1] * width, 2 * weight.shape[1] * width),
        name="row_own",
    )(first, pre, weight)


def row_rest_kernel(first_ref, own_ref, mine_ref, pre_ref, w_ref, *out_refs):
    half = (pre_ref.shape[1] - LANES) // 2
    width = own_ref.shape[1]
    start = pl.multiple_of(first_ref[0], half)
    total = (
        own_ref[...]
        + jnp.dot(pre_ref[:, :half], w_ref[0, pl.ds(start, half), :], preferred_element_type=F32)
        + jnp.dot(
            pre_ref[:, half : 2 * half], w_ref[1, pl.ds(start, half), :], preferred_element_type=F32
        )
    )
    lanes = mine_ref[:, 2 * half :].astype(F32) + pre_ref[:, 2 * half :].astype(F32)
    route = lanes[:, 0:1] + lanes[:, 1:2]
    at = 0
    for out in out_refs:
        rows = out.shape[0]
        out[:, :width] = total[at : at + rows].astype(out.dtype)
        if out.dtype == F32:
            out[:, width:] = jnp.broadcast_to(route[at : at + rows], (rows, LANES)) * jnp.where(
                lax.broadcasted_iota(jnp.int32, (rows, LANES), 1) == 0, 1.0, 0.0
            )
        else:
            out[:, width:] = high_low(route[at : at + rows])
        at += rows


def row_rest(own, mine, pre, weight, first, outs):
    rows, width = own.shape
    return pl.pallas_call(
        row_rest_kernel,
        in_specs=[SMEM] + [VMEM] * 4,
        out_specs=[VMEM] * len(outs),
        out_shape=[jax.ShapeDtypeStruct((n, width + LANES), kind) for n, kind in outs],
        compiler_params=params(24),
        cost_estimate=cost(2 * rows * weight.shape[1] * width, 2 * weight.shape[1] * width),
        name="row_rest",
    )(first, own, mine, pre, weight)


def write_tiles(tiles, make, out_at, buf, sem):
    ring = buf.shape[0]
    copies = []
    for i, tile in enumerate(tiles):
        slot = i % ring
        if i >= ring:
            copies[i - ring].wait()
        buf[slot] = make(tile)
        copy = pltpu.make_async_copy(buf.at[slot], out_at(tile), sem.at[slot])
        copy.start()
        copies.append(copy)
    for copy in copies[max(0, len(copies) - ring) :]:
        copy.wait()


def grad_out_kernel(nblocks, first_ref, mine_ref, peer_ref, *refs):
    blocks = refs[:nblocks]
    out_ref, cot, buf, sem = refs[nblocks:]
    width = out_ref.shape[1]
    half = mine_ref.shape[1]
    step = buf.shape[1]
    at = 0
    for b in blocks:
        rows = b.shape[0]
        cot[at : at + rows, :] = (
            b[:, width : width + 1].astype(F32) * b[:, :width].astype(F32)
        ).astype(BF16)
        at += rows
    starts = (pl.multiple_of(first_ref[0], half), pl.multiple_of(first_ref[1], half))
    sources = (mine_ref, peer_ref)
    tiles = [(s, j) for s in range(2) for j in range(0, half, step)]

    def make(tile):
        s, j = tile
        return lax.dot_general(
            sources[s][:, j : j + step], cot[...], TN, preferred_element_type=F32
        )

    def out_at(tile):
        s, j = tile
        return out_ref.at[pl.ds(starts[s] + j, step)]

    write_tiles(tiles, make, out_at, buf, sem)


def grad_out(mine, peer, blocks, firsts, width):
    rows, half = mine.shape
    step = min(half, 256)
    ring = min(8, 2 * half // step)
    return pl.pallas_call(
        functools.partial(grad_out_kernel, len(blocks)),
        in_specs=[SMEM] + [VMEM] * (2 + len(blocks)),
        out_specs=ANY,
        out_shape=jax.ShapeDtypeStruct((2 * half, width), F32),
        scratch_shapes=[
            pltpu.VMEM((rows, width), BF16),
            pltpu.VMEM((ring, step, width), F32),
            pltpu.SemaphoreType.DMA((ring,)),
        ],
        compiler_params=params(28),
        cost_estimate=cost(4 * rows * half * width, 8 * half * width),
        name="grad_out",
    )(firsts, mine, peer, *blocks)


def grad_in_kernel(nblocks, first_ref, mine_ref, peer_ref, *refs):
    blocks = refs[:nblocks]
    out_ref, tok, buf, sem = refs[nblocks:]
    half = (mine_ref.shape[1] - LANES) // 2
    step = buf.shape[1]
    at = 0
    for b in blocks:
        rows = b.shape[0]
        tok[at : at + rows, :] = b[...]
        at += rows
    starts = (pl.multiple_of(first_ref[0], half), pl.multiple_of(first_ref[1], half))
    sources = (mine_ref, peer_ref)
    tiles = [(s, c, j) for s in range(2) for c in range(2) for j in range(0, half, step)]

    def make(tile):
        s, c, j = tile
        at = c * half + j
        return lax.dot_general(
            sources[s][:, at : at + step], tok[...], TN, preferred_element_type=F32
        )

    def out_at(tile):
        s, c, j = tile
        return out_ref.at[c, pl.ds(starts[s] + j, step)]

    write_tiles(tiles, make, out_at, buf, sem)


def grad_in(mine, peer, blocks, firsts, width):
    rows = mine.shape[0]
    half = (mine.shape[1] - LANES) // 2
    step = min(half, 256)
    ring = min(8, 4 * half // step)
    return pl.pallas_call(
        functools.partial(grad_in_kernel, len(blocks)),
        in_specs=[SMEM] + [VMEM] * (2 + len(blocks)),
        out_specs=ANY,
        out_shape=jax.ShapeDtypeStruct((2, 2 * half, width), F32),
        scratch_shapes=[
            pltpu.VMEM((rows, width), BF16),
            pltpu.VMEM((ring, step, width), F32),
            pltpu.SemaphoreType.DMA((ring,)),
        ],
        compiler_params=params(28),
        cost_estimate=cost(8 * rows * half * width, 16 * half * width),
        name="grad_in",
    )(firsts, mine, peer, *blocks)


def place_kernel(nblocks, ids_ref, *refs):
    blocks, (in_ref, weight_ref) = refs[:nblocks], refs[nblocks:]
    width = in_ref.shape[1]
    capacity = blocks[0].shape[0]
    total = sum(b[:, :width].astype(F32) for b in blocks)
    lanes = sum(b[:, width:].astype(F32) for b in blocks)
    ids = ids_ref[...]
    picker = slot_selector(ids, capacity).astype(BF16)
    in_ref[...] = jnp.dot(picker, total.astype(BF16), preferred_element_type=F32).astype(BF16)
    route = jnp.broadcast_to(lanes[:, 0:1] + lanes[:, 1:2], (capacity, LANES))
    high = route.astype(BF16)
    low = (route - high.astype(F32)).astype(BF16)
    spread = jnp.dot(picker, high, preferred_element_type=F32) + jnp.dot(
        picker, low, preferred_element_type=F32
    )
    weight_ref[...] = jnp.where(ids == 0, spread[:, : ids.shape[1]], 0.0).astype(BF16)


def place(expert_ids, blocks):
    tok_rows = expert_ids.shape[0]
    width = blocks[0].shape[1] - LANES
    return pl.pallas_call(
        functools.partial(place_kernel, len(blocks)),
        in_specs=[VMEM] * (1 + len(blocks)),
        out_specs=[VMEM] * 2,
        out_shape=[
            jax.ShapeDtypeStruct((tok_rows, width), BF16),
            jax.ShapeDtypeStruct(expert_ids.shape, BF16),
        ],
        compiler_params=params(8),
        name="place",
    )(expert_ids, *blocks)


def swap(array, axis, size, distance):
    return lax.ppermute(array, axis, [(i, i ^ distance) for i in range(size)])


def per_device(dp, chips, tokens, cotangent, expert_ids, quantized, weight_in, weight_out):
    experts = 2 * chips
    width = tokens.shape[1]
    hidden = weight_in.shape[1]
    half = hidden // 2
    core = lax.rem(lax.axis_index("expert"), 2)
    own = (core * half).astype(jnp.int32).reshape(1)
    other = ((1 - core) * half).astype(jnp.int32).reshape(1)
    firsts = jnp.concatenate([own, other])
    direct = dp == 4

    weight_out = weight_out.reshape((1,) + weight_out.shape)
    send_in, send_grad = select(tokens, cotangent, expert_ids, quantized)
    if direct:
        tok_blocks = [send_in] + [swap(send_in, "dp", dp, d) for d in range(1, dp)]
        cot_blocks = [send_grad] + [swap(send_grad, "dp", dp, d) for d in range(1, dp)]
        groups = [tok_blocks[:2], tok_blocks[2:]]
    else:
        tok_blocks = [lax.all_gather(send_in, "dp", axis=0, tiled=True)]
        cot_blocks = [lax.all_gather(send_grad, "dp", axis=0, tiled=True)]
        groups = [tok_blocks]

    weight_in = pltpu.with_memory_space_constraint(weight_in, pltpu.VMEM)
    weight_out = pltpu.with_memory_space_constraint(weight_out, pltpu.VMEM)

    def summed(blocks, weight):
        theirs = project(blocks, weight, other, BF16)
        arrived = swap(theirs, "expert", experts, 1)
        mine = project(blocks, weight, own, F32)
        chip = (mine + arrived.astype(F32)).astype(BF16)
        return [chip] + [swap(chip, "expert", experts, 2 * k) for k in range(1, chips)]

    gu = [summed(blocks, weight_in) for blocks in groups]
    back = summed(cot_blocks, weight_out)

    units = hidden_units(gu)
    units_peer = swap(units, "expert", experts, 1)
    grad_weight_out = grad_out(units, units_peer, cot_blocks, firsts, width)

    pre = pre_grads(gu, back, cot_blocks, width)
    pre_peer = swap(pre, "expert", experts, 1)
    part = row_own(pre, weight_in, own)
    if direct:
        cap = send_in.shape[0]
        outs = [(cap, F32)] + [(cap, BF16)] * (dp - 1)
        sent = row_rest(part, pre, pre_peer, weight_in, other, outs)
        arrived = [sent[0]] + [swap(sent[d], "dp", dp, d) for d in range(1, dp)]
    else:
        sent = row_rest(part, pre, pre_peer, weight_in, other, [(part.shape[0], F32)])
        arrived = [lax.psum_scatter(sent[0], "dp", scatter_dimension=0, tiled=True)]
    grad_weight_in = grad_in(pre, pre_peer, tok_blocks, firsts, width)
    input_grad, weight_grad = place(expert_ids, arrived)
    return (input_grad, weight_grad, grad_weight_in, grad_weight_out)


def solution(mesh):
    return jax.shard_map(
        functools.partial(per_device, mesh.shape["dp"], mesh.shape["expert"] // 2),
        mesh=mesh,
        in_specs=(
            P(("group", "dp"), "expert"),
            P(("group", "dp"), "expert"),
            P(("group", "dp"), None),
            P(("group", "dp"), None),
            P(None, "dp", "expert"),
            P("dp", "expert"),
        ),
        out_specs=(
            P(("group", "dp"), "expert"),
            P(("group", "dp"), None),
            P("group", "dp", "expert"),
            P(("group", "dp"), "expert"),
        ),
        check_vma=False,
    )
```

```python
import functools

import jax
import jax.numpy as jnp
from jax import lax
from jax.experimental import pallas as pl
from jax.experimental.pallas import tpu as pltpu
from jax.sharding import PartitionSpec as P

F32 = jnp.float32
BF16 = jnp.bfloat16
VMEM = pl.BlockSpec(memory_space=pltpu.VMEM)
SMEM = pl.BlockSpec(memory_space=pltpu.SMEM)
ANY = pl.BlockSpec(memory_space=pl.ANY)
HBM = pl.BlockSpec(memory_space=pltpu.HBM)
LANES = 128
MIB = 2**20

NT = (((1,), (1,)), ((), ()))
TN = (((0,), (0,)), ((), ()))


def params(mib):
    return pltpu.CompilerParams(vmem_limit_bytes=mib * MIB)


def in_hbm(array):
    return pltpu.with_memory_space_constraint(array, pltpu.HBM)


def in_vmem(array):
    return pltpu.with_memory_space_constraint(array, pltpu.VMEM)


STEP = pl.CostEstimate(flops=7 * 10**9, bytes_accessed=1024, transcendentals=0)
FIRST = pl.CostEstimate(flops=12 * 10**9, bytes_accessed=1024, transcendentals=0)


def fetch(pairs, sems):
    copies = [pltpu.make_async_copy(a, b, sems.at[i]) for i, (a, b) in enumerate(pairs)]
    for copy in copies:
        copy.start()
    for copy in copies:
        copy.wait()


def load_kernel(pieces, *refs):
    w_ref, out_ref, sems = refs[0], refs[-2], refs[-1]
    kinds, hidden, _ = w_ref.shape
    step = hidden // pieces
    spans = [(k, pl.ds(j * step, step)) for k in range(kinds) for j in range(pieces)]
    fetch([(w_ref.at[s], out_ref.at[s]) for s in spans], sems)


def load(weight, after):
    kinds, pieces = weight.shape[0], 4
    return pl.pallas_call(
        functools.partial(load_kernel, pieces),
        in_specs=[HBM] + [ANY] * len(after),
        out_specs=VMEM,
        out_shape=pltpu.VMEM(weight.shape, weight.dtype),
        scratch_shapes=[pltpu.SemaphoreType.DMA((kinds * pieces,))],
        compiler_params=params(8),
        cost_estimate=STEP,
        name="load",
    )(in_hbm(weight), *after)


def slot_picker(ids, capacity):
    tok_rows = ids.shape[1]
    routed = jnp.logical_or(ids[0:1] == 0, ids[1:2] == 0)
    row = lax.broadcasted_iota(jnp.int32, (tok_rows, tok_rows), 0)
    col = lax.broadcasted_iota(jnp.int32, (tok_rows, tok_rows), 1)
    before = jnp.where(row < col, 1.0, 0.0).astype(BF16)
    flags = jnp.broadcast_to(jnp.where(routed, 1.0, 0.0), (capacity, tok_rows))
    position = jnp.dot(flags.astype(BF16), before, preferred_element_type=F32)
    slot = lax.broadcasted_iota(jnp.int32, (capacity, tok_rows), 0).astype(F32)
    return jnp.where(position == slot, flags, 0.0).astype(BF16)


def select_tokens_kernel(own_ref, other_ref, tok_hbm, ids_hbm, out_ref, tok_ref, ids_ref, sems):
    del own_ref, other_ref
    fetch([(tok_hbm, tok_ref), (ids_hbm, ids_ref)], sems)
    picker = slot_picker(ids_ref[...], out_ref.shape[0])
    out_ref[...] = jnp.dot(picker, tok_ref[...], preferred_element_type=F32).astype(BF16)


def select_tokens(firsts, tokens, expert_ids):
    capacity, width = tokens.shape[0] // 4, tokens.shape[1]
    return pl.pallas_call(
        select_tokens_kernel,
        in_specs=[SMEM] * 2 + [HBM] * 2,
        out_specs=VMEM,
        out_shape=jax.ShapeDtypeStruct((capacity, width), BF16),
        scratch_shapes=[pltpu.VMEM(a.shape, a.dtype) for a in (tokens, expert_ids)]
        + [pltpu.SemaphoreType.DMA((2,))],
        compiler_params=params(8),
        cost_estimate=FIRST,
        name="select",
    )(*firsts, *(in_hbm(a) for a in (tokens, expert_ids)))


def select_cotangent_kernel(after_ref, cot_hbm, ids_hbm, quant_hbm, out_ref, *scratch):
    del after_ref
    cot_ref, ids_ref, quant_ref, sems = scratch
    fetch([(cot_hbm, cot_ref), (ids_hbm, ids_ref), (quant_hbm, quant_ref)], sems)
    capacity, width = out_ref.shape[0], cot_ref.shape[1]
    ids = ids_ref[...]
    picker = slot_picker(ids, capacity)
    scaled = quant_ref[...].astype(F32)
    total = scaled[0:1] + scaled[1:2]
    routing = (scaled / total).astype(BF16).astype(F32)
    weight = jnp.where(ids == 0, routing, 0.0)
    rate = jnp.broadcast_to(weight[0:1] + weight[1:2], (LANES, ids.shape[1])).astype(BF16)
    out_ref[:, :width] = jnp.dot(picker, cot_ref[...], preferred_element_type=F32).astype(BF16)
    out_ref[:, width:] = lax.dot_general(picker, rate, NT, preferred_element_type=F32).astype(BF16)


def select_cotangent(after, cotangent, expert_ids, quantized):
    capacity, width = cotangent.shape[0] // 4, cotangent.shape[1]
    arrays = (cotangent, expert_ids, quantized)
    return pl.pallas_call(
        select_cotangent_kernel,
        in_specs=[ANY] + [HBM] * 3,
        out_specs=VMEM,
        out_shape=jax.ShapeDtypeStruct((capacity, width + LANES), BF16),
        scratch_shapes=[pltpu.VMEM(a.shape, a.dtype) for a in arrays]
        + [pltpu.SemaphoreType.DMA((3,))],
        compiler_params=params(8),
        cost_estimate=STEP,
        name="select_cot",
    )(after, *(in_hbm(a) for a in arrays))


def project_kernel(nblocks, width, offset, first_ref, *refs):
    blocks, w_ref, out_ref = refs[:nblocks], refs[nblocks], refs[-1]
    kinds = w_ref.shape[0]
    units = out_ref.shape[1] // kinds
    rows = jnp.concatenate([b[:, :width] for b in blocks], axis=0)
    start = pl.multiple_of(first_ref[0] + offset, units)
    step = min(units, 512)
    for kind in range(kinds):
        for j in range(0, units, step):
            out_ref[:, kind * units + j : kind * units + j + step] = lax.dot_general(
                rows, w_ref[kind, pl.ds(start + j, step), :], NT, preferred_element_type=F32
            ).astype(out_ref.dtype)


def project(blocks, weight, first, span, out_type, after=()):
    kinds, _, width = weight.shape
    offset, units = span
    rows = sum(b.shape[0] for b in blocks)
    return pl.pallas_call(
        functools.partial(project_kernel, len(blocks), width, offset),
        in_specs=[SMEM] + [VMEM] * (len(blocks) + 1) + [ANY] * len(after),
        out_specs=VMEM,
        out_shape=jax.ShapeDtypeStruct((rows, kinds * units), out_type),
        compiler_params=params(24),
        cost_estimate=STEP,
        name="project",
    )(first, *blocks, in_vmem(weight), *after)


def gated(sums):
    half = sums.shape[1] // 2
    gate, up = sums[:, :half], sums[:, half:]
    return gate, up, jax.nn.sigmoid(gate)


def hidden_kernel(nparts, *refs):
    out_ref = refs[-1]
    gate, up, s = gated(sum(p[...].astype(F32) for p in refs[:nparts]))
    out_ref[...] = (gate * s * up).astype(BF16)


def hidden_units(parts, after=()):
    rows, units = parts[0].shape[0], parts[0].shape[1] // 2
    return pl.pallas_call(
        functools.partial(hidden_kernel, len(parts)),
        in_specs=[VMEM] * len(parts) + [ANY] * len(after),
        out_specs=VMEM,
        out_shape=jax.ShapeDtypeStruct((rows, units), BF16),
        compiler_params=params(16),
        cost_estimate=STEP,
        name="hidden",
    )(*parts, *after)


def pre_kernel(nchunks, nparts, nblocks, width, *refs):
    chunks = [refs[i * nparts : (i + 1) * nparts] for i in range(nchunks)]
    back_parts = refs[nchunks * nparts :][:nparts]
    blocks = refs[(nchunks + 1) * nparts :][:nblocks]
    out_ref = refs[-1]
    half = back_parts[0].shape[1]
    rate = jnp.concatenate([b[:, width : width + 1].astype(F32) for b in blocks], axis=0)
    route = jnp.zeros_like(rate)
    at = 0
    for parts in chunks:
        gate, up, s = gated(sum(p[...].astype(F32) for p in parts))
        units = gate.shape[1]
        back = sum(p[:, at : at + units].astype(F32) for p in back_parts)
        hidden = (gate * s * up).astype(BF16).astype(F32)
        route += jnp.sum(hidden * back, axis=1, keepdims=True)
        grad = rate * back
        gate_grad = grad * up * s * (1.0 + gate * (1.0 - s))
        up_grad = grad * gate * s
        out_ref[:, at : at + units] = gate_grad.astype(BF16)
        out_ref[:, half + at : half + at + units] = up_grad.astype(BF16)
        at += units
    out_ref[:, 2 * half :] = high_low(route)


def high_low(value):
    high = value.astype(BF16).astype(F32)
    low = value - high
    lane = lax.broadcasted_iota(jnp.int32, (value.shape[0], LANES), 1)
    return jnp.where(lane == 0, high, jnp.where(lane == 1, low, 0.0)).astype(BF16)


def pre_grads(groups, back_parts, blocks, width, after=()):
    half = back_parts[0].shape[1]
    rows = back_parts[0].shape[0]
    flat = [p for g in groups for p in g]
    return pl.pallas_call(
        functools.partial(pre_kernel, len(groups), len(groups[0]), len(blocks), width),
        in_specs=[VMEM] * (len(flat) + len(back_parts) + len(blocks)) + [ANY] * len(after),
        out_specs=VMEM,
        out_shape=jax.ShapeDtypeStruct((rows, 2 * half + LANES), BF16),
        compiler_params=params(16),
        cost_estimate=STEP,
        name="pre",
    )(*flat, *back_parts, *blocks, *after)


def row_own_kernel(first_ref, pre_ref, w_ref, out_ref):
    half = (pre_ref.shape[1] - LANES) // 2
    start = pl.multiple_of(first_ref[0], half)
    out_ref[...] = jnp.dot(
        pre_ref[:, :half], w_ref[0, pl.ds(start, half), :], preferred_element_type=F32
    ) + jnp.dot(
        pre_ref[:, half : 2 * half], w_ref[1, pl.ds(start, half), :], preferred_element_type=F32
    )


def row_own(pre, weight, first):
    rows, width = pre.shape[0], weight.shape[2]
    return pl.pallas_call(
        row_own_kernel,
        in_specs=[SMEM, VMEM, VMEM],
        out_specs=VMEM,
        out_shape=jax.ShapeDtypeStruct((rows, width), F32),
        compiler_params=params(24),
        cost_estimate=STEP,
        name="row_own",
    )(first, pre, in_vmem(weight))


def row_rest_kernel(first_ref, own_ref, mine_ref, pre_ref, w_ref, *out_refs):
    half = (pre_ref.shape[1] - LANES) // 2
    width = own_ref.shape[1]
    start = pl.multiple_of(first_ref[0], half)
    total = (
        own_ref[...]
        + jnp.dot(pre_ref[:, :half], w_ref[0, pl.ds(start, half), :], preferred_element_type=F32)
        + jnp.dot(
            pre_ref[:, half : 2 * half], w_ref[1, pl.ds(start, half), :], preferred_element_type=F32
        )
    )
    lanes = mine_ref[:, 2 * half :].astype(F32) + pre_ref[:, 2 * half :].astype(F32)
    route = lanes[:, 0:1] + lanes[:, 1:2]
    at = 0
    for out in out_refs:
        rows = out.shape[0]
        out[:, :width] = total[at : at + rows].astype(out.dtype)
        if out.dtype == F32:
            out[:, width:] = jnp.broadcast_to(route[at : at + rows], (rows, LANES)) * jnp.where(
                lax.broadcasted_iota(jnp.int32, (rows, LANES), 1) == 0, 1.0, 0.0
            )
        else:
            out[:, width:] = high_low(route[at : at + rows])
        at += rows


def row_rest(own, mine, pre, weight, first, outs):
    rows, width = own.shape
    return pl.pallas_call(
        row_rest_kernel,
        in_specs=[SMEM] + [VMEM] * 4,
        out_specs=[VMEM] * len(outs),
        out_shape=[jax.ShapeDtypeStruct((n, width + LANES), kind) for n, kind in outs],
        compiler_params=params(24),
        cost_estimate=STEP,
        name="row_rest",
    )(first, own, mine, pre, in_vmem(weight))


def write_tiles(tiles, make, out_at, buf, sem):
    ring = buf.shape[0]
    copies = []
    for i, tile in enumerate(tiles):
        slot = i % ring
        if i >= ring:
            copies[i - ring].wait()
        buf[slot] = make(tile)
        copy = pltpu.make_async_copy(buf.at[slot], out_at(tile), sem.at[slot])
        copy.start()
        copies.append(copy)
    for copy in copies[max(0, len(copies) - ring) :]:
        copy.wait()


def grad_out_kernel(nblocks, places, nafter, own_ref, other_ref, *refs):
    sources, blocks = refs[: len(places)], refs[len(places) :][:nblocks]
    out_ref, mark_ref, cot, buf, sem = refs[len(places) + nblocks + nafter :]
    mark_ref[...] = jnp.zeros_like(mark_ref)
    width = out_ref.shape[1]
    half = out_ref.shape[0] // 2
    step = buf.shape[1]
    at = 0
    for b in blocks:
        rows = b.shape[0]
        cot[at : at + rows, :] = (
            b[:, width : width + 1].astype(F32) * b[:, :width].astype(F32)
        ).astype(BF16)
        at += rows
    starts = (pl.multiple_of(own_ref[0], half), pl.multiple_of(other_ref[0], half))
    tiles = [(s, j) for s in range(len(places)) for j in range(0, sources[s].shape[1], step)]

    def make(tile):
        s, j = tile
        return lax.dot_general(
            sources[s][:, j : j + step], cot[...], TN, preferred_element_type=F32
        )

    def out_at(tile):
        s, j = tile
        side, offset = places[s]
        return out_ref.at[pl.ds(starts[side] + offset + j, step)]

    write_tiles(tiles, make, out_at, buf, sem)


def grad_out(pieces, blocks, firsts, hidden, width, so_far, after=()):
    sources = [piece[0] for piece in pieces]
    places = [piece[1:] for piece in pieces]
    rows, units = sources[0].shape
    step = min(units, 256)
    ring = min(8, len(sources) * units // step)
    before = [] if so_far is None else [in_hbm(so_far)]
    return pl.pallas_call(
        functools.partial(grad_out_kernel, len(blocks), places, len(after) + len(before)),
        in_specs=[SMEM] * 2
        + [VMEM] * (len(sources) + len(blocks))
        + [ANY] * len(after)
        + [HBM] * len(before),
        out_specs=[HBM, VMEM],
        out_shape=[
            pltpu.HBM((hidden, width), F32),
            jax.ShapeDtypeStruct((8, LANES), F32),
        ],
        scratch_shapes=[
            pltpu.VMEM((rows, width), BF16),
            pltpu.VMEM((ring, step, width), F32),
            pltpu.SemaphoreType.DMA((ring,)),
        ],
        input_output_aliases=(
            {2 + len(sources) + len(blocks) + len(after): 0} if before else {}
        ),
        compiler_params=params(28),
        cost_estimate=STEP,
        name="grad_out",
    )(*firsts, *sources, *blocks, *after, *before)


def grad_in_kernel(nblocks, own_ref, other_ref, mine_ref, peer_ref, *refs):
    blocks = refs[:nblocks]
    out_ref, tok, buf, sem = refs[nblocks:]
    half = (mine_ref.shape[1] - LANES) // 2
    step = buf.shape[1]
    at = 0
    for b in blocks:
        rows = b.shape[0]
        tok[at : at + rows, :] = b[...]
        at += rows
    starts = (pl.multiple_of(own_ref[0], half), pl.multiple_of(other_ref[0], half))
    sources = (mine_ref, peer_ref)
    tiles = [(s, c, j) for s in range(2) for c in range(2) for j in range(0, half, step)]

    def make(tile):
        s, c, j = tile
        at = c * half + j
        return lax.dot_general(
            sources[s][:, at : at + step], tok[...], TN, preferred_element_type=F32
        )

    def out_at(tile):
        s, c, j = tile
        return out_ref.at[c, pl.ds(starts[s] + j, step)]

    write_tiles(tiles, make, out_at, buf, sem)


def grad_in(mine, peer, blocks, firsts, width):
    rows = mine.shape[0]
    half = (mine.shape[1] - LANES) // 2
    step = min(half, 256)
    ring = min(8, 4 * half // step)
    return pl.pallas_call(
        functools.partial(grad_in_kernel, len(blocks)),
        in_specs=[SMEM] * 2 + [VMEM] * (2 + len(blocks)),
        out_specs=HBM,
        out_shape=pltpu.HBM((2, 2 * half, width), F32),
        scratch_shapes=[
            pltpu.VMEM((rows, width), BF16),
            pltpu.VMEM((ring, step, width), F32),
            pltpu.SemaphoreType.DMA((ring,)),
        ],
        compiler_params=params(28),
        cost_estimate=STEP,
        name="grad_in",
    )(*firsts, mine, peer, *blocks)


def place_kernel(nblocks, ids_ref, *refs):
    blocks, (in_ref, weight_ref) = refs[:nblocks], refs[nblocks:]
    width = in_ref.shape[1]
    capacity = blocks[0].shape[0]
    total = sum(b[:, :width].astype(F32) for b in blocks)
    lanes = sum(b[:, width:].astype(F32) for b in blocks)
    ids = ids_ref[...]
    picker = slot_picker(ids, capacity)
    in_ref[...] = lax.dot_general(
        picker, total.astype(BF16), TN, preferred_element_type=F32
    ).astype(BF16)
    route = jnp.broadcast_to(lanes[:, 0:1] + lanes[:, 1:2], (capacity, LANES))
    high = route.astype(BF16)
    low = (route - high.astype(F32)).astype(BF16)
    spread = lax.dot_general(high, picker, TN, preferred_element_type=F32) + lax.dot_general(
        low, picker, TN, preferred_element_type=F32
    )
    weight_ref[...] = jnp.where(ids == 0, spread[: ids.shape[0]], 0.0).astype(BF16)


def place(expert_ids, blocks):
    tok_rows = expert_ids.shape[1]
    width = blocks[0].shape[1] - LANES
    return pl.pallas_call(
        functools.partial(place_kernel, len(blocks)),
        in_specs=[VMEM] * (1 + len(blocks)),
        out_specs=[VMEM] * 2,
        out_shape=[
            jax.ShapeDtypeStruct((tok_rows, width), BF16),
            jax.ShapeDtypeStruct(expert_ids.shape, BF16),
        ],
        compiler_params=params(8),
        cost_estimate=STEP,
        name="place",
    )(expert_ids, *blocks)


def swap(array, axis, size, distance):
    return lax.ppermute(array, axis, [(i, i ^ distance) for i in range(size)])


def relay_kernel(block_ref, after_ref, out_ref):
    del after_ref
    out_ref[...] = block_ref[...]


def relay(block, after):
    return pl.pallas_call(
        relay_kernel,
        in_specs=[VMEM, ANY],
        out_specs=VMEM,
        out_shape=jax.ShapeDtypeStruct(block.shape, block.dtype),
        compiler_params=params(8),
        cost_estimate=STEP,
        name="relay",
    )(block, after)


def per_device(dp, chips, tokens, cotangent, expert_ids, quantized, weight_in, weight_out):
    experts = 2 * chips
    width = tokens.shape[1]
    hidden = weight_in.shape[1]
    half = hidden // 2
    core = lax.rem(lax.axis_index("expert"), 2)
    firsts = [(c * half).astype(jnp.int32).reshape(1) for c in (core, 1 - core)]
    direct = dp == 4

    expert_ids, quantized = expert_ids.T, quantized.T
    weight_out = weight_out.reshape((1,) + weight_out.shape)
    send_in = select_tokens(firsts, tokens, expert_ids)
    if direct:
        across = swap(send_in, "dp", dp, 2)
        tok_blocks = [send_in, swap(send_in, "dp", dp, 1), across, swap(across, "dp", dp, 1)]
        send_grad = select_cotangent(across, cotangent, expert_ids, quantized)
        cot_blocks = [send_grad, swap(send_grad, "dp", dp, 1), swap(send_grad, "dp", dp, 2)]
    else:
        send_grad = select_cotangent(send_in, cotangent, expert_ids, quantized)
        tok_blocks = [lax.all_gather(send_in, "dp", axis=0, tiled=True)]
        cot_blocks = [lax.all_gather(send_grad, "dp", axis=0, tiled=True)]

    def summed(blocks, weight, span, after=()):
        theirs = project(blocks, weight, firsts[1], span, BF16, after)
        arrived = swap(theirs, "expert", experts, 1)
        mine = project(blocks, weight, firsts[0], span, F32, [theirs])
        chip = (mine + arrived.astype(F32)).astype(BF16)
        return theirs, [chip] + [swap(chip, "expert", experts, 2 * k) for k in range(1, chips)]

    pieces = 2 if half % 256 == 0 else 1
    units = half // pieces
    gu, last = [], send_grad
    for i in range(pieces):
        theirs, parts = summed(tok_blocks, weight_in, (i * units, units), [last])
        gu.append(parts)
        last = parts[0]
    if direct:
        cot_blocks.append(swap(relay(cot_blocks[2], theirs), "dp", dp, 1))
    _, back = summed(cot_blocks, weight_out, (0, half), [last])

    grad_weight_out, last, waiting = None, back[0], []
    for i, parts in enumerate(gu):
        mine = hidden_units(parts, [last])
        ready = waiting + [(mine, 0, i * units)]
        grad_weight_out, last = grad_out(ready, cot_blocks, firsts, hidden, width, grad_weight_out)
        waiting = [(swap(mine, "expert", experts, 1), 1, i * units)]
    grad_weight_out, mark = grad_out(
        waiting, cot_blocks, firsts, hidden, width, grad_weight_out, [last]
    )

    pre = pre_grads(gu, back, cot_blocks, width, [mark])
    pre_peer = swap(pre, "expert", experts, 1)
    part = row_own(pre, weight_in, firsts[0])
    if direct:
        cap = send_in.shape[0]
        outs = [(cap, F32)] + [(cap, BF16)] * (dp - 1)
        sent = row_rest(part, pre, pre_peer, weight_in, firsts[1], outs)
        arrived = [sent[0]] + [swap(sent[d], "dp", dp, d) for d in range(1, dp)]
    else:
        sent = row_rest(part, pre, pre_peer, weight_in, firsts[1], [(part.shape[0], F32)])
        arrived = [lax.psum_scatter(sent[0], "dp", scatter_dimension=0, tiled=True)]
    grad_weight_in = grad_in(pre, pre_peer, tok_blocks, firsts, width)
    input_grad, weight_grad = place(expert_ids, arrived)
    return (input_grad, weight_grad.T, grad_weight_in, grad_weight_out)


def solution(mesh):
    return jax.shard_map(
        functools.partial(per_device, mesh.shape["dp"], mesh.shape["expert"] // 2),
        mesh=mesh,
        in_specs=(
            P(("group", "dp"), "expert"),
            P(("group", "dp"), "expert"),
            P(("group", "dp"), None),
            P(("group", "dp"), None),
            P(None, "dp", "expert"),
            P("dp", "expert"),
        ),
        out_specs=(
            P(("group", "dp"), "expert"),
            P(("group", "dp"), None),
            P("group", "dp", "expert"),
            P(("group", "dp"), "expert"),
        ),
        check_vma=False,
    )
```

```python
import functools

import jax
import jax.numpy as jnp
from jax import lax
from jax.experimental import pallas as pl
from jax.experimental.pallas import tpu as pltpu
from jax.sharding import PartitionSpec as P

F32 = jnp.float32
BF16 = jnp.bfloat16
VMEM = pl.BlockSpec(memory_space=pltpu.VMEM)
SMEM = pl.BlockSpec(memory_space=pltpu.SMEM)
ANY = pl.BlockSpec(memory_space=pl.ANY)
HBM = pl.BlockSpec(memory_space=pltpu.HBM)
LANES = 128
MIB = 2**20

NT = (((1,), (1,)), ((), ()))
TN = (((0,), (0,)), ((), ()))


def params(mib):
    return pltpu.CompilerParams(vmem_limit_bytes=mib * MIB)


def in_hbm(array):
    return pltpu.with_memory_space_constraint(array, pltpu.HBM)


def in_vmem(array):
    return pltpu.with_memory_space_constraint(array, pltpu.VMEM)


STEP = pl.CostEstimate(flops=7 * 10**9, bytes_accessed=1024, transcendentals=0)
FIRST = pl.CostEstimate(flops=12 * 10**9, bytes_accessed=1024, transcendentals=0)


def fetch(pairs, sems):
    copies = [pltpu.make_async_copy(a, b, sems.at[i]) for i, (a, b) in enumerate(pairs)]
    for copy in copies:
        copy.start()
    for copy in copies:
        copy.wait()


def slot_picker(ids, capacity):
    tok_rows = ids.shape[1]
    routed = jnp.logical_or(ids[0:1] == 0, ids[1:2] == 0)
    row = lax.broadcasted_iota(jnp.int32, (tok_rows, tok_rows), 0)
    col = lax.broadcasted_iota(jnp.int32, (tok_rows, tok_rows), 1)
    before = jnp.where(row < col, 1.0, 0.0).astype(BF16)
    flags = jnp.broadcast_to(jnp.where(routed, 1.0, 0.0), (capacity, tok_rows))
    position = jnp.dot(flags.astype(BF16), before, preferred_element_type=F32)
    slot = lax.broadcasted_iota(jnp.int32, (capacity, tok_rows), 0).astype(F32)
    return jnp.where(position == slot, flags, 0.0).astype(BF16)


def select_kernel(own_ref, other_ref, *refs):
    del own_ref, other_ref
    sources, (in_ref, grad_ref, picker_ref), scratch, sems = refs[:4], refs[4:7], refs[7:11], refs[11]
    fetch(zip(sources, scratch), sems)
    tok_ref, cot_ref, ids_ref, quant_ref = scratch
    capacity, width = in_ref.shape
    ids = ids_ref[...]
    picker = slot_picker(ids, capacity)
    picker_ref[...] = picker
    in_ref[...] = jnp.dot(picker, tok_ref[...], preferred_element_type=F32).astype(BF16)
    scaled = quant_ref[...].astype(F32)
    total = scaled[0:1] + scaled[1:2]
    routing = (scaled / total).astype(BF16).astype(F32)
    weight = jnp.where(ids == 0, routing, 0.0)
    rate = jnp.broadcast_to(weight[0:1] + weight[1:2], (LANES, ids.shape[1])).astype(BF16)
    grad_ref[:, :width] = jnp.dot(picker, cot_ref[...], preferred_element_type=F32).astype(BF16)
    grad_ref[:, width:] = lax.dot_general(picker, rate, NT, preferred_element_type=F32).astype(BF16)


def select(firsts, *arrays):
    tok_rows, width = arrays[0].shape
    capacity = tok_rows // 4
    return pl.pallas_call(
        select_kernel,
        in_specs=[SMEM] * 2 + [HBM] * 4,
        out_specs=[VMEM] * 3,
        out_shape=[
            jax.ShapeDtypeStruct((capacity, width), BF16),
            jax.ShapeDtypeStruct((capacity, width + LANES), BF16),
            jax.ShapeDtypeStruct((capacity, tok_rows), BF16),
        ],
        scratch_shapes=[pltpu.VMEM(a.shape, a.dtype) for a in arrays]
        + [pltpu.SemaphoreType.DMA((4,))],
        compiler_params=params(8),
        cost_estimate=FIRST,
        name="select",
    )(*firsts, *(in_hbm(a) for a in arrays))


def project_kernel(nblocks, width, units, first_ref, *refs):
    blocks, w_ref, out_ref = refs[:nblocks], refs[nblocks], refs[-1]
    kinds = w_ref.shape[0]
    half = out_ref.shape[1] // kinds
    rows = jnp.concatenate([b[:, :width] for b in blocks], axis=0)
    start = pl.multiple_of(first_ref[0], half)
    step = min(units, 512)
    at = 0
    for piece in range(0, half, units):
        for kind in range(kinds):
            for j in range(piece, piece + units, step):
                out_ref[:, at : at + step] = lax.dot_general(
                    rows, w_ref[kind, pl.ds(start + j, step), :], NT, preferred_element_type=F32
                ).astype(out_ref.dtype)
                at += step


def project(blocks, weight, first, units, out_type, after):
    kinds, hidden, width = weight.shape
    rows = sum(b.shape[0] for b in blocks)
    return pl.pallas_call(
        functools.partial(project_kernel, len(blocks), width, units),
        in_specs=[SMEM] + [VMEM] * (len(blocks) + 1) + [ANY] * len(after),
        out_specs=VMEM,
        out_shape=jax.ShapeDtypeStruct((rows, kinds * hidden // 2), out_type),
        compiler_params=params(24),
        cost_estimate=STEP,
        name="project",
    )(first, *blocks, in_vmem(weight), *after)


def add_kernel(mine_ref, arrived_ref, *out_refs):
    at = 0
    for out in out_refs:
        cut = slice(at, at + out.shape[1])
        out[...] = (mine_ref[:, cut] + arrived_ref[:, cut].astype(F32)).astype(BF16)
        at = cut.stop


def add(mine, arrived, cuts):
    rows, columns = mine.shape
    return pl.pallas_call(
        add_kernel,
        in_specs=[VMEM] * 2,
        out_specs=[VMEM] * cuts,
        out_shape=[jax.ShapeDtypeStruct((rows, columns // cuts), BF16)] * cuts,
        compiler_params=params(16),
        cost_estimate=STEP,
        name="add",
    )(mine, arrived)


def gate_up(refs, layout, units):
    at = 0
    for nparts, column in layout:
        parts, refs = refs[:nparts], refs[nparts:]
        sums = sum(p[:, column : column + 2 * units].astype(F32) for p in parts)
        yield slice(at, at + sums.shape[0]), sums[:, :units], sums[:, units:]
        at += sums.shape[0]


def hidden_kernel(layout, *refs):
    out_ref = refs[-1]
    for here, gate, up in gate_up(refs, layout, out_ref.shape[1]):
        out_ref[here, :] = (gate * jax.nn.sigmoid(gate) * up).astype(BF16)


def hidden_units(groups, units, after):
    flat = [p for parts, _ in groups for p in parts]
    rows = sum(parts[0].shape[0] for parts, _ in groups)
    return pl.pallas_call(
        functools.partial(hidden_kernel, [(len(parts), column) for parts, column in groups]),
        in_specs=[VMEM] * len(flat) + [ANY] * len(after),
        out_specs=VMEM,
        out_shape=jax.ShapeDtypeStruct((rows, units), BF16),
        compiler_params=params(16),
        cost_estimate=STEP,
        name="hidden",
    )(*flat, *after)


def pre_kernel(layouts, nback, nblocks, width, *refs):
    nsums = sum(n for layout in layouts for n, _ in layout)
    back_parts = refs[nsums : nsums + nback]
    blocks = refs[nsums + nback :][:nblocks]
    out_ref = refs[-1]
    half = back_parts[0].shape[1]
    units = half // len(layouts)
    rates = jnp.concatenate([b[:, width : width + 1].astype(F32) for b in blocks], axis=0)
    routes = {}
    for i, layout in enumerate(layouts):
        first, second = slice(i * units, (i + 1) * units), slice(half + i * units, half + (i + 1) * units)
        for here, gate, up in gate_up(refs, layout, units):
            s = jax.nn.sigmoid(gate)
            back = sum(p[here, first].astype(F32) for p in back_parts)
            hidden = (gate * s * up).astype(BF16).astype(F32)
            route = jnp.sum(hidden * back, axis=1, keepdims=True)
            routes[here.start] = routes[here.start] + route if i else route
            grad = rates[here] * back
            out_ref[here, first] = (grad * up * s * (1.0 + gate * (1.0 - s))).astype(BF16)
            out_ref[here, second] = (grad * gate * s).astype(BF16)
            if i == len(layouts) - 1:
                out_ref[here, 2 * half :] = high_low(routes[here.start])
        refs = refs[sum(n for n, _ in layout) :]


def high_low(value):
    high = value.astype(BF16).astype(F32)
    low = value - high
    lane = lax.broadcasted_iota(jnp.int32, (value.shape[0], LANES), 1)
    return jnp.where(lane == 0, high, jnp.where(lane == 1, low, 0.0)).astype(BF16)


def pre_grads(chunks, back_parts, blocks, width, after):
    half = back_parts[0].shape[1]
    rows = back_parts[0].shape[0]
    flat = [p for groups in chunks for parts, _ in groups for p in parts]
    layouts = [[(len(parts), column) for parts, column in groups] for groups in chunks]
    return pl.pallas_call(
        functools.partial(pre_kernel, layouts, len(back_parts), len(blocks), width),
        in_specs=[VMEM] * (len(flat) + len(back_parts) + len(blocks)) + [ANY] * len(after),
        out_specs=VMEM,
        out_shape=jax.ShapeDtypeStruct((rows, 2 * half + LANES), BF16),
        compiler_params=params(16),
        cost_estimate=STEP,
        name="pre",
    )(*flat, *back_parts, *blocks, *after)


def row_part(pre_ref, w_ref, start):
    half = (pre_ref.shape[1] - LANES) // 2
    return sum(
        jnp.dot(
            pre_ref[:, k * half : (k + 1) * half],
            w_ref[k, pl.ds(start, half), :],
            preferred_element_type=F32,
        )
        for k in range(2)
    )


def row_rest_kernel(first_ref, own_ref, mine_ref, pre_ref, w_ref, *out_refs):
    half = (pre_ref.shape[1] - LANES) // 2
    width = own_ref.shape[1]
    start = pl.multiple_of(first_ref[0], half)
    total = (
        own_ref[...]
        + jnp.dot(pre_ref[:, :half], w_ref[0, pl.ds(start, half), :], preferred_element_type=F32)
        + jnp.dot(
            pre_ref[:, half : 2 * half], w_ref[1, pl.ds(start, half), :], preferred_element_type=F32
        )
    )
    lanes = mine_ref[:, 2 * half :].astype(F32) + pre_ref[:, 2 * half :].astype(F32)
    route = lanes[:, 0:1] + lanes[:, 1:2]
    at = 0
    for out in out_refs:
        rows = out.shape[0]
        out[:, :width] = total[at : at + rows].astype(out.dtype)
        if out.dtype == F32:
            out[:, width:] = jnp.broadcast_to(route[at : at + rows], (rows, LANES)) * jnp.where(
                lax.broadcasted_iota(jnp.int32, (rows, LANES), 1) == 0, 1.0, 0.0
            )
        else:
            out[:, width:] = high_low(route[at : at + rows])
        at += rows


def row_rest(own, mine, pre, weight, first, outs):
    rows, width = own.shape
    return pl.pallas_call(
        row_rest_kernel,
        in_specs=[SMEM] + [VMEM] * 4,
        out_specs=[VMEM] * len(outs),
        out_shape=[jax.ShapeDtypeStruct((n, width + LANES), kind) for n, kind in outs],
        compiler_params=params(24),
        cost_estimate=STEP,
        name="row_rest",
    )(first, own, mine, pre, in_vmem(weight))


def grads_kernel(outs, nin, ntok, ncot, nrows, nafter, nbefore, own_ref, other_ref, *refs):
    out_sources, refs = refs[: len(outs)], refs[len(outs) :]
    in_sources, refs = refs[:nin], refs[nin:]
    toks, refs = refs[:ntok], refs[ntok:]
    cots, refs = refs[:ncot], refs[ncot:]
    summed, refs = refs[:nrows], refs[nrows:]
    refs = refs[nafter + nbefore :]
    out_ref, *extra, rows_of, buf, sem = refs
    hidden, width = out_ref.shape[-2:]
    half = hidden // 2
    ring, step = buf.shape[:2]
    at = 0
    for t in toks:
        rows_of[at : at + t.shape[0], :] = t[...]
        at += t.shape[0]
    for c in cots:
        rows_of[at : at + c.shape[0], :] = (
            c[:, width : width + 1].astype(F32) * c[:, :width].astype(F32)
        ).astype(BF16)
        at += c.shape[0]
    starts = [pl.multiple_of(ref[0], half) for ref in (own_ref, other_ref)]
    tiles = []
    for source, (side, offset) in zip(out_sources, outs):
        for j in range(0, source.shape[1], step):
            tiles.append((source, j, out_ref.at[pl.ds(starts[side] + offset + j, step)]))
    for side, source in enumerate(in_sources):
        for kind in range(2):
            for j in range(0, half, step):
                target = out_ref.at[kind, pl.ds(starts[side] + j, step)]
                tiles.append((source, kind * half + j, target))
    copies = []
    for i, (source, column, target) in enumerate(tiles):
        if i >= ring:
            copies[i - ring].wait()
        buf[i % ring] = lax.dot_general(
            source[:, column : column + step], rows_of[...], TN, preferred_element_type=F32
        )
        copies.append(pltpu.make_async_copy(buf.at[i % ring], target, sem.at[i % ring]))
        copies[-1].start()
    for more in extra:
        more[...] = row_part(*summed, starts[0]) if summed else jnp.zeros_like(more)
    for copy in copies[max(0, len(copies) - ring) :]:
        copy.wait()


def grads(outs, ins, tok_blocks, cot_blocks, firsts, hidden, so_far, after=(), extra=None):
    width = tok_blocks[0].shape[1] if ins else cot_blocks[0].shape[1] - LANES
    sources = [piece[0] for piece in outs]
    places = [piece[1:] for piece in outs]
    rows = (sources + list(ins))[0].shape[0]
    units = [source.shape[1] for source in sources] + [hidden // 2 for _ in ins]
    step = min(units + [256])
    ring = min(8, (sum(units) + sum(units[len(sources) :])) // step)
    before = [] if so_far is None else [in_hbm(so_far)]
    toks = tok_blocks if ins else []
    shape = (2, hidden, width) if ins else (hidden, width)
    out_shape = [pltpu.HBM(shape, F32)]
    summed = []
    if extra == ():
        out_shape.append(jax.ShapeDtypeStruct((8, LANES), F32))
    elif extra:
        out_shape.append(jax.ShapeDtypeStruct((rows, width), F32))
        summed = [extra[0], in_vmem(extra[1])]
    operands = [*sources, *ins, *toks, *cot_blocks, *summed]
    sizes = (len(ins), len(toks), len(cot_blocks), len(summed), len(after), len(before))
    return pl.pallas_call(
        functools.partial(grads_kernel, places, *sizes),
        in_specs=[SMEM] * 2 + [VMEM] * len(operands) + [ANY] * len(after) + [HBM] * len(before),
        out_specs=[HBM] + [VMEM] * (len(out_shape) - 1),
        out_shape=out_shape,
        scratch_shapes=[
            pltpu.VMEM((rows, width), BF16),
            pltpu.VMEM((ring, step, width), F32),
            pltpu.SemaphoreType.DMA((ring,)),
        ],
        input_output_aliases=(
            {2 + len(operands) + len(after): 0} if before else {}
        ),
        compiler_params=params(28),
        cost_estimate=STEP,
        name="grads",
    )(*firsts, *operands, *after, *before)


def place_kernel(ids_ref, picker_ref, *refs):
    blocks, (in_ref, weight_ref) = refs[:-2], refs[-2:]
    width = in_ref.shape[1]
    capacity = picker_ref.shape[0]
    picker = picker_ref[...]
    total = sum(b[:, :width].astype(F32) for b in blocks)
    lanes = sum(b[:, width:].astype(F32) for b in blocks)
    in_ref[...] = lax.dot_general(
        picker, total.astype(BF16), TN, preferred_element_type=F32
    ).astype(BF16)
    route = jnp.broadcast_to(lanes[:, 0:1] + lanes[:, 1:2], (capacity, LANES))
    high = route.astype(BF16)
    low = (route - high.astype(F32)).astype(BF16)
    spread = lax.dot_general(high, picker, TN, preferred_element_type=F32) + lax.dot_general(
        low, picker, TN, preferred_element_type=F32
    )
    ids = ids_ref[...]
    weight_ref[...] = jnp.where(ids == 0, spread[: ids.shape[0]], 0.0).astype(BF16)


def place(expert_ids, picker, blocks):
    width = blocks[0].shape[1] - LANES
    return pl.pallas_call(
        place_kernel,
        in_specs=[VMEM] * (2 + len(blocks)),
        out_specs=[VMEM] * 2,
        out_shape=[
            jax.ShapeDtypeStruct((picker.shape[1], width), BF16),
            jax.ShapeDtypeStruct(expert_ids.shape, BF16),
        ],
        compiler_params=params(8),
        cost_estimate=STEP,
        name="place",
    )(expert_ids, picker, *blocks)


def swap(array, axis, size, distance):
    return lax.ppermute(array, axis, [(i, i ^ distance) for i in range(size)])


def relay_kernel(nblocks, *refs):
    blocks, out_ref = refs[:nblocks], refs[-1]
    at = 0
    for b in blocks:
        out_ref[at : at + b.shape[0], :] = b[...]
        at += b.shape[0]


def relay(blocks, after):
    rows = sum(b.shape[0] for b in blocks)
    return pl.pallas_call(
        functools.partial(relay_kernel, len(blocks)),
        in_specs=[VMEM] * len(blocks) + [ANY],
        out_specs=VMEM,
        out_shape=jax.ShapeDtypeStruct((rows, blocks[0].shape[1]), blocks[0].dtype),
        compiler_params=params(8),
        cost_estimate=STEP,
        name="relay",
    )(*blocks, after)


def per_device(dp, chips, tokens, cotangent, expert_ids, quantized, weight_in, weight_out):
    experts = 2 * chips
    width = tokens.shape[1]
    hidden = weight_in.shape[1]
    half = hidden // 2
    core = lax.rem(lax.axis_index("expert"), 2)
    firsts = [(c * half).astype(jnp.int32).reshape(1) for c in (core, 1 - core)]
    direct = dp == 4

    expert_ids, quantized = expert_ids.T, quantized.T
    weight_out = weight_out.reshape((1,) + weight_out.shape)
    send_in, send_grad, picker = select(firsts, tokens, cotangent, expert_ids, quantized)
    if direct:
        tok_blocks = [send_in] + [swap(send_in, "dp", dp, d) for d in range(1, dp)]
        cot_blocks = [send_grad] + [swap(send_grad, "dp", dp, d) for d in (1, 2)]
        groups = [tok_blocks[:2], tok_blocks[2:]]
    else:
        tok_blocks = [lax.all_gather(send_in, "dp", axis=0, tiled=True)]
        cot_blocks = [lax.all_gather(send_grad, "dp", axis=0, tiled=True)]
        groups = [tok_blocks]

    pieces, units = 1, half

    def chip_sums(blocks, weight, last, cuts=1, meanwhile=None):
        theirs = project(blocks, weight, firsts[1], units, BF16, [last])
        arrived = swap(theirs, "expert", experts, 1)
        last = meanwhile(theirs) if meanwhile is not None else theirs
        mine = project(blocks, weight, firsts[0], units, F32, [last])
        return add(mine, arrived, cuts)

    def all_chips(chip):
        return [chip] + [swap(chip, "expert", experts, 2 * k) for k in range(1, chips)]

    def pass_on(after):
        block = relay([send_grad], after)
        cot_blocks.append(swap(block, "dp", dp, 3))
        return block

    chunks, last = [[] for _ in range(pieces)], send_grad
    for blocks in groups[:-1]:
        (last,) = chip_sums(blocks, weight_in, last)
        parts = all_chips(last)
        for i, groups_of in enumerate(chunks):
            groups_of.append((parts, i * 2 * units))
    if direct:
        last = pass_on(last)
    cuts = chip_sums(groups[-1], weight_in, last, pieces)
    for groups_of, cut in zip(chunks, cuts):
        groups_of.append((all_chips(cut), 0))
    back = all_chips(*chip_sums(cot_blocks, weight_out, cuts[-1]))

    mine = hidden_units(chunks[0], units, [back[0]])
    peer = swap(mine, "expert", experts, 1)
    grad_weight_out, last = grads(
        [(mine, 0, 0)], [], [], cot_blocks, firsts, hidden, None, extra=()
    )
    pre = pre_grads(chunks, back, cot_blocks, width, [last])
    pre_peer = swap(pre, "expert", experts, 1)
    grad_weight_out, part = grads(
        [(peer, 1, 0)],
        [],
        [],
        cot_blocks,
        firsts,
        hidden,
        grad_weight_out,
        extra=(pre, weight_in),
    )
    if direct:
        cap = send_in.shape[0]
        outs = [(cap, F32)] + [(cap, BF16)] * (dp - 1)
        sent = row_rest(part, pre, pre_peer, weight_in, firsts[1], outs)
        arrived = [sent[0]] + [swap(sent[d], "dp", dp, d) for d in (2, 3, 1)]
    else:
        sent = row_rest(part, pre, pre_peer, weight_in, firsts[1], [(part.shape[0], F32)])
        arrived = [lax.psum_scatter(sent[0], "dp", scatter_dimension=0, tiled=True)]
    (grad_weight_in,) = grads(
        [],
        [pre, pre_peer],
        tok_blocks,
        [],
        firsts,
        hidden,
        None,
        [sent[0]],
    )
    input_grad, weight_grad = place(expert_ids, picker, arrived)
    return (input_grad, weight_grad.T, grad_weight_in, grad_weight_out)


def solution(mesh):
    return jax.shard_map(
        functools.partial(per_device, mesh.shape["dp"], mesh.shape["expert"] // 2),
        mesh=mesh,
        in_specs=(
            P(("group", "dp"), "expert"),
            P(("group", "dp"), "expert"),
            P(("group", "dp"), None),
            P(("group", "dp"), None),
            P(None, "dp", "expert"),
            P("dp", "expert"),
        ),
        out_specs=(
            P(("group", "dp"), "expert"),
            P(("group", "dp"), None),
            P("group", "dp", "expert"),
            P(("group", "dp"), "expert"),
        ),
        check_vma=False,
    )
```

```python
import functools

import jax
import jax.numpy as jnp
from jax import lax
from jax.experimental import pallas as pl
from jax.experimental.pallas import tpu as pltpu
from jax.sharding import PartitionSpec as P

F32 = jnp.float32
BF16 = jnp.bfloat16
VMEM = pl.BlockSpec(memory_space=pltpu.VMEM)
SMEM = pl.BlockSpec(memory_space=pltpu.SMEM)
ANY = pl.BlockSpec(memory_space=pl.ANY)
HBM = pl.BlockSpec(memory_space=pltpu.HBM)
LANES = 128
MIB = 2**20

NT = (((1,), (1,)), ((), ()))
TN = (((0,), (0,)), ((), ()))


def params(mib):
    return pltpu.CompilerParams(vmem_limit_bytes=mib * MIB)


def in_hbm(array):
    return pltpu.with_memory_space_constraint(array, pltpu.HBM)


def in_vmem(array):
    return pltpu.with_memory_space_constraint(array, pltpu.VMEM)


STEP = pl.CostEstimate(flops=16 * 10**9, bytes_accessed=1024, transcendentals=0)
FIRST = pl.CostEstimate(flops=18 * 10**9, bytes_accessed=1024, transcendentals=0)


def slot_picker(ids, capacity):
    tok_rows = ids.shape[1]
    routed = jnp.logical_or(ids[0:1] == 0, ids[1:2] == 0)
    row = lax.broadcasted_iota(jnp.int32, (tok_rows, tok_rows), 0)
    col = lax.broadcasted_iota(jnp.int32, (tok_rows, tok_rows), 1)
    before = jnp.where(row < col, 1.0, 0.0).astype(BF16)
    flags = jnp.broadcast_to(jnp.where(routed, 1.0, 0.0), (capacity, tok_rows))
    position = jnp.dot(flags.astype(BF16), before, preferred_element_type=F32)
    slot = lax.broadcasted_iota(jnp.int32, (capacity, tok_rows), 0).astype(F32)
    return jnp.where(position == slot, flags, 0.0).astype(BF16)


def select_kernel(own_ref, other_ref, *refs):
    del own_ref, other_ref
    sources, (in_ref, grad_ref, picker_ref), scratch, sems = refs[:4], refs[4:7], refs[7:11], refs[11]
    copies = [
        pltpu.make_async_copy(a, b, sems.at[i]) for i, (a, b) in enumerate(zip(sources, scratch))
    ]
    for copy in reversed(copies):
        copy.start()
    tok_ref, cot_ref, ids_ref, quant_ref = scratch
    copies[2].wait()
    copies[3].wait()
    capacity, width = in_ref.shape
    ids = ids_ref[...]
    picker = slot_picker(ids, capacity)
    picker_ref[...] = picker
    scaled = quant_ref[...].astype(F32)
    total = scaled[0:1] + scaled[1:2]
    routing = (scaled / total).astype(BF16).astype(F32)
    weight = jnp.where(ids == 0, routing, 0.0)
    rate = jnp.broadcast_to(weight[0:1] + weight[1:2], (LANES, ids.shape[1])).astype(BF16)
    grad_ref[:, width:] = lax.dot_general(picker, rate, NT, preferred_element_type=F32).astype(BF16)
    copies[0].wait()
    in_ref[...] = jnp.dot(picker, tok_ref[...], preferred_element_type=F32).astype(BF16)
    copies[1].wait()
    grad_ref[:, :width] = jnp.dot(picker, cot_ref[...], preferred_element_type=F32).astype(BF16)


def select(firsts, *arrays):
    tok_rows, width = arrays[0].shape
    capacity = tok_rows // 4
    return pl.pallas_call(
        select_kernel,
        in_specs=[SMEM] * 2 + [HBM] * 4,
        out_specs=[VMEM] * 3,
        out_shape=[
            jax.ShapeDtypeStruct((capacity, width), BF16),
            jax.ShapeDtypeStruct((capacity, width + LANES), BF16),
            jax.ShapeDtypeStruct((capacity, tok_rows), BF16),
        ],
        scratch_shapes=[pltpu.VMEM(a.shape, a.dtype) for a in arrays]
        + [pltpu.SemaphoreType.DMA((4,))],
        compiler_params=params(8),
        cost_estimate=FIRST,
        name="select",
    )(*firsts, *(in_hbm(a) for a in arrays))


def project_kernel(nblocks, width, units, first_ref, *refs):
    blocks, w_ref, out_ref = refs[:nblocks], refs[nblocks], refs[-1]
    kinds = w_ref.shape[0]
    half = out_ref.shape[1] // kinds
    rows = jnp.concatenate([b[:, :width] for b in blocks], axis=0)
    start = pl.multiple_of(first_ref[0], half)
    step = min(units, 512)
    at = 0
    for piece in range(0, half, units):
        for kind in range(kinds):
            for j in range(piece, piece + units, step):
                out_ref[:, at : at + step] = lax.dot_general(
                    rows, w_ref[kind, pl.ds(start + j, step), :], NT, preferred_element_type=F32
                ).astype(out_ref.dtype)
                at += step


def project(blocks, weight, first, units, out_type, after):
    kinds, hidden, width = weight.shape
    rows = sum(b.shape[0] for b in blocks)
    return pl.pallas_call(
        functools.partial(project_kernel, len(blocks), width, units),
        in_specs=[SMEM] + [VMEM] * (len(blocks) + 1) + [ANY] * len(after),
        out_specs=VMEM,
        out_shape=jax.ShapeDtypeStruct((rows, kinds * hidden // 2), out_type),
        compiler_params=params(24),
        cost_estimate=STEP,
        name="project",
    )(first, *blocks, in_vmem(weight), *after)


def add_kernel(mine_ref, arrived_ref, *out_refs):
    at = 0
    for out in out_refs:
        cut = slice(at, at + out.shape[1])
        out[...] = (mine_ref[:, cut] + arrived_ref[:, cut].astype(F32)).astype(BF16)
        at = cut.stop


def add(mine, arrived, cuts):
    rows, columns = mine.shape
    return pl.pallas_call(
        add_kernel,
        in_specs=[VMEM] * 2,
        out_specs=[VMEM] * cuts,
        out_shape=[jax.ShapeDtypeStruct((rows, columns // cuts), BF16)] * cuts,
        compiler_params=params(16),
        cost_estimate=STEP,
        name="add",
    )(mine, arrived)


def gate_up(refs, layout, units):
    at = 0
    for nparts, column in layout:
        parts, refs = refs[:nparts], refs[nparts:]
        sums = sum(p[:, column : column + 2 * units].astype(F32) for p in parts)
        yield slice(at, at + sums.shape[0]), sums[:, :units], sums[:, units:]
        at += sums.shape[0]


def hidden_kernel(layout, *refs):
    out_ref = refs[-1]
    for here, gate, up in gate_up(refs, layout, out_ref.shape[1]):
        out_ref[here, :] = (gate * jax.nn.sigmoid(gate) * up).astype(BF16)


def hidden_units(groups, units, after):
    flat = [p for parts, _ in groups for p in parts]
    rows = sum(parts[0].shape[0] for parts, _ in groups)
    return pl.pallas_call(
        functools.partial(hidden_kernel, [(len(parts), column) for parts, column in groups]),
        in_specs=[VMEM] * len(flat) + [ANY] * len(after),
        out_specs=VMEM,
        out_shape=jax.ShapeDtypeStruct((rows, units), BF16),
        compiler_params=params(16),
        cost_estimate=STEP,
        name="hidden",
    )(*flat, *after)


def pre_kernel(layouts, nback, nblocks, width, *refs):
    nsums = sum(n for layout in layouts for n, _ in layout)
    back_parts = refs[nsums : nsums + nback]
    blocks = refs[nsums + nback :][:nblocks]
    out_ref = refs[-1]
    half = back_parts[0].shape[1]
    units = half // len(layouts)
    rates = jnp.concatenate([b[:, width : width + 1].astype(F32) for b in blocks], axis=0)
    routes = {}
    for i, layout in enumerate(layouts):
        first, second = slice(i * units, (i + 1) * units), slice(half + i * units, half + (i + 1) * units)
        for here, gate, up in gate_up(refs, layout, units):
            s = jax.nn.sigmoid(gate)
            back = sum(p[here, first].astype(F32) for p in back_parts)
            hidden = (gate * s * up).astype(BF16).astype(F32)
            route = jnp.sum(hidden * back, axis=1, keepdims=True)
            routes[here.start] = routes[here.start] + route if i else route
            grad = rates[here] * back
            out_ref[here, first] = (grad * up * s * (1.0 + gate * (1.0 - s))).astype(BF16)
            out_ref[here, second] = (grad * gate * s).astype(BF16)
            if i == len(layouts) - 1:
                out_ref[here, 2 * half :] = high_low(routes[here.start])
        refs = refs[sum(n for n, _ in layout) :]


def high_low(value):
    high = value.astype(BF16).astype(F32)
    low = value - high
    lane = lax.broadcasted_iota(jnp.int32, (value.shape[0], LANES), 1)
    return jnp.where(lane == 0, high, jnp.where(lane == 1, low, 0.0)).astype(BF16)


def pre_grads(chunks, back_parts, blocks, width, after):
    half = back_parts[0].shape[1]
    rows = back_parts[0].shape[0]
    flat = [p for groups in chunks for parts, _ in groups for p in parts]
    layouts = [[(len(parts), column) for parts, column in groups] for groups in chunks]
    return pl.pallas_call(
        functools.partial(pre_kernel, layouts, len(back_parts), len(blocks), width),
        in_specs=[VMEM] * (len(flat) + len(back_parts) + len(blocks)) + [ANY] * len(after),
        out_specs=VMEM,
        out_shape=jax.ShapeDtypeStruct((rows, 2 * half + LANES), BF16),
        compiler_params=params(16),
        cost_estimate=STEP,
        name="pre",
    )(*flat, *back_parts, *blocks, *after)


def row_part(pre_ref, w_ref, start):
    half = (pre_ref.shape[1] - LANES) // 2
    return sum(
        jnp.dot(
            pre_ref[:, k * half : (k + 1) * half],
            w_ref[k, pl.ds(start, half), :],
            preferred_element_type=F32,
        )
        for k in range(2)
    )


def row_rest_kernel(first_ref, own_ref, mine_ref, pre_ref, w_ref, *out_refs):
    half = (pre_ref.shape[1] - LANES) // 2
    width = own_ref.shape[1]
    start = pl.multiple_of(first_ref[0], half)
    total = (
        own_ref[...]
        + jnp.dot(pre_ref[:, :half], w_ref[0, pl.ds(start, half), :], preferred_element_type=F32)
        + jnp.dot(
            pre_ref[:, half : 2 * half], w_ref[1, pl.ds(start, half), :], preferred_element_type=F32
        )
    )
    lanes = mine_ref[:, 2 * half :].astype(F32) + pre_ref[:, 2 * half :].astype(F32)
    route = lanes[:, 0:1] + lanes[:, 1:2]
    at = 0
    for out in out_refs:
        rows = out.shape[0]
        out[:, :width] = total[at : at + rows].astype(out.dtype)
        if out.dtype == F32:
            out[:, width:] = jnp.broadcast_to(route[at : at + rows], (rows, LANES)) * jnp.where(
                lax.broadcasted_iota(jnp.int32, (rows, LANES), 1) == 0, 1.0, 0.0
            )
        else:
            out[:, width:] = high_low(route[at : at + rows])
        at += rows


def row_rest(own, mine, pre, weight, first, outs):
    rows, width = own.shape
    return pl.pallas_call(
        row_rest_kernel,
        in_specs=[SMEM] + [VMEM] * 4,
        out_specs=[VMEM] * len(outs),
        out_shape=[jax.ShapeDtypeStruct((n, width + LANES), kind) for n, kind in outs],
        compiler_params=params(24),
        cost_estimate=STEP,
        name="row_rest",
    )(first, own, mine, pre, in_vmem(weight))


def grads_kernel(outs, nin, ntok, ncot, nrows, nafter, nbefore, own_ref, other_ref, *refs):
    out_sources, refs = refs[: len(outs)], refs[len(outs) :]
    in_sources, refs = refs[:nin], refs[nin:]
    toks, refs = refs[:ntok], refs[ntok:]
    cots, refs = refs[:ncot], refs[ncot:]
    summed, refs = refs[:nrows], refs[nrows:]
    refs = refs[nafter + nbefore :]
    out_ref, *extra, rows_of, buf, sem = refs
    hidden, width = out_ref.shape[-2:]
    half = hidden // 2
    ring, step = buf.shape[:2]
    at = 0
    for t in toks:
        rows_of[at : at + t.shape[0], :] = t[...]
        at += t.shape[0]
    for c in cots:
        rows_of[at : at + c.shape[0], :] = (
            c[:, width : width + 1].astype(F32) * c[:, :width].astype(F32)
        ).astype(BF16)
        at += c.shape[0]
    starts = [pl.multiple_of(ref[0], half) for ref in (own_ref, other_ref)]
    tiles = []
    for source, (side, first, end) in zip(out_sources, outs):
        for j in range(first, end, step):
            tiles.append((source, j, out_ref.at[pl.ds(starts[side] + j, step)]))
    for side, source in enumerate(in_sources):
        for kind in range(2):
            for j in range(0, half, step):
                target = out_ref.at[kind, pl.ds(starts[side] + j, step)]
                tiles.append((source, kind * half + j, target))
    copies = []
    for i, (source, column, target) in enumerate(tiles):
        if i >= ring:
            copies[i - ring].wait()
        buf[i % ring] = lax.dot_general(
            source[:, column : column + step], rows_of[...], TN, preferred_element_type=F32
        )
        copies.append(pltpu.make_async_copy(buf.at[i % ring], target, sem.at[i % ring]))
        copies[-1].start()
    for more in extra:
        more[...] = row_part(*summed, starts[0]) if summed else jnp.zeros_like(more)
    for copy in copies[max(0, len(copies) - ring) :]:
        copy.wait()


def grads(outs, ins, tok_blocks, cot_blocks, firsts, hidden, so_far, after=(), extra=None):
    width = tok_blocks[0].shape[1] if ins else cot_blocks[0].shape[1] - LANES
    sources = [piece[0] for piece in outs]
    places = [piece[1:] for piece in outs]
    rows = (sources + list(ins))[0].shape[0]
    step = min(hidden // 2, 256)
    ring = min(8, (sum(end - first for _, first, end in places) + len(ins) * hidden) // step)
    before = [] if so_far is None else [in_hbm(so_far)]
    toks = tok_blocks if ins else []
    shape = (2, hidden, width) if ins else (hidden, width)
    out_shape = [pltpu.HBM(shape, F32)]
    summed = []
    if extra == ():
        out_shape.append(jax.ShapeDtypeStruct((8, LANES), F32))
    elif extra:
        out_shape.append(jax.ShapeDtypeStruct((rows, width), F32))
        summed = [extra[0], in_vmem(extra[1])]
    operands = [*sources, *ins, *toks, *cot_blocks, *summed]
    sizes = (len(ins), len(toks), len(cot_blocks), len(summed), len(after), len(before))
    return pl.pallas_call(
        functools.partial(grads_kernel, places, *sizes),
        in_specs=[SMEM] * 2 + [VMEM] * len(operands) + [ANY] * len(after) + [HBM] * len(before),
        out_specs=[HBM] + [VMEM] * (len(out_shape) - 1),
        out_shape=out_shape,
        scratch_shapes=[
            pltpu.VMEM((rows, width), BF16),
            pltpu.VMEM((ring, step, width), F32),
            pltpu.SemaphoreType.DMA((ring,)),
        ],
        input_output_aliases=(
            {2 + len(operands) + len(after): 0} if before else {}
        ),
        compiler_params=params(28),
        cost_estimate=STEP,
        name="grads",
    )(*firsts, *operands, *after, *before)


def place_kernel(ids_ref, picker_ref, *refs):
    blocks, (in_ref, weight_ref) = refs[:-2], refs[-2:]
    width = in_ref.shape[1]
    capacity = picker_ref.shape[0]
    picker = picker_ref[...]
    total = sum(b[:, :width].astype(F32) for b in blocks)
    lanes = sum(b[:, width:].astype(F32) for b in blocks)
    in_ref[...] = lax.dot_general(
        picker, total.astype(BF16), TN, preferred_element_type=F32
    ).astype(BF16)
    route = jnp.broadcast_to(lanes[:, 0:1] + lanes[:, 1:2], (capacity, LANES))
    high = route.astype(BF16)
    low = (route - high.astype(F32)).astype(BF16)
    spread = lax.dot_general(high, picker, TN, preferred_element_type=F32) + lax.dot_general(
        low, picker, TN, preferred_element_type=F32
    )
    ids = ids_ref[...]
    weight_ref[...] = jnp.where(ids == 0, spread[: ids.shape[0]], 0.0).astype(BF16)


def place(expert_ids, picker, blocks):
    width = blocks[0].shape[1] - LANES
    return pl.pallas_call(
        place_kernel,
        in_specs=[VMEM] * (2 + len(blocks)),
        out_specs=[VMEM] * 2,
        out_shape=[
            jax.ShapeDtypeStruct((picker.shape[1], width), BF16),
            jax.ShapeDtypeStruct(expert_ids.shape, BF16),
        ],
        compiler_params=params(8),
        cost_estimate=STEP,
        name="place",
    )(expert_ids, picker, *blocks)


def swap(array, axis, size, distance):
    return lax.ppermute(array, axis, [(i, i ^ distance) for i in range(size)])


def relay_kernel(nblocks, *refs):
    blocks, out_ref = refs[:nblocks], refs[-1]
    at = 0
    for b in blocks:
        out_ref[at : at + b.shape[0], :] = b[...]
        at += b.shape[0]


def relay(blocks, after):
    rows = sum(b.shape[0] for b in blocks)
    return pl.pallas_call(
        functools.partial(relay_kernel, len(blocks)),
        in_specs=[VMEM] * len(blocks) + [ANY],
        out_specs=VMEM,
        out_shape=jax.ShapeDtypeStruct((rows, blocks[0].shape[1]), blocks[0].dtype),
        compiler_params=params(8),
        cost_estimate=STEP,
        name="relay",
    )(*blocks, after)


def per_device(dp, chips, tokens, cotangent, expert_ids, quantized, weight_in, weight_out):
    experts = 2 * chips
    width = tokens.shape[1]
    hidden = weight_in.shape[1]
    half = hidden // 2
    core = lax.rem(lax.axis_index("expert"), 2)
    firsts = [(c * half).astype(jnp.int32).reshape(1) for c in (core, 1 - core)]
    direct = dp == 4

    expert_ids, quantized = expert_ids.T, quantized.T
    weight_out = weight_out.reshape((1,) + weight_out.shape)
    send_in, send_grad, picker = select(firsts, tokens, cotangent, expert_ids, quantized)
    if direct:
        tok_blocks = [send_in] + [swap(send_in, "dp", dp, d) for d in range(1, dp)]
        cot_blocks = [send_grad] + [swap(send_grad, "dp", dp, d) for d in (1, 2)]
        groups = [tok_blocks[:2], tok_blocks[2:]]
    else:
        tok_blocks = [lax.all_gather(send_in, "dp", axis=0, tiled=True)]
        cot_blocks = [lax.all_gather(send_grad, "dp", axis=0, tiled=True)]
        groups = [tok_blocks]

    pieces, units = 1, half

    def chip_sums(blocks, weight, last, cuts=1, meanwhile=None):
        theirs = project(blocks, weight, firsts[1], units, BF16, [last])
        arrived = swap(theirs, "expert", experts, 1)
        last = meanwhile(theirs) if meanwhile is not None else theirs
        mine = project(blocks, weight, firsts[0], units, F32, [last])
        return add(mine, arrived, cuts)

    def all_chips(chip):
        return [chip] + [swap(chip, "expert", experts, 2 * k) for k in range(1, chips)]

    def pass_on(after):
        block = relay([send_grad], after)
        cot_blocks.append(swap(block, "dp", dp, 3))
        return block

    chunks, last = [[] for _ in range(pieces)], send_grad
    for blocks in groups[:-1]:
        (last,) = chip_sums(blocks, weight_in, last)
        parts = all_chips(last)
        for i, groups_of in enumerate(chunks):
            groups_of.append((parts, i * 2 * units))
    if direct:
        last = pass_on(last)
    cuts = chip_sums(groups[-1], weight_in, last, pieces)
    for groups_of, cut in zip(chunks, cuts):
        groups_of.append((all_chips(cut), 0))
    back = all_chips(*chip_sums(cot_blocks, weight_out, cuts[-1]))

    mine = hidden_units(chunks[0], units, [back[0]])
    peer = swap(mine, "expert", experts, 1)
    middle = half // 2 if half % 512 == 0 else 0
    grad_weight_out, *mark = grads(
        [(mine, 0, 0, half)],
        [],
        [],
        cot_blocks,
        firsts,
        hidden,
        None,
        extra=None if middle else (),
    )
    if middle:
        grad_weight_out, *mark = grads(
            [(peer, 1, 0, middle)], [], [], cot_blocks, firsts, hidden, grad_weight_out, extra=()
        )
    pre = pre_grads(chunks, back, cot_blocks, width, mark)
    pre_peer = swap(pre, "expert", experts, 1)
    grad_weight_out, part = grads(
        [(peer, 1, middle, half)],
        [],
        [],
        cot_blocks,
        firsts,
        hidden,
        grad_weight_out,
        extra=(pre, weight_in),
    )
    if direct:
        cap = send_in.shape[0]
        outs = [(cap, F32)] + [(cap, BF16)] * (dp - 1)
        sent = row_rest(part, pre, pre_peer, weight_in, firsts[1], outs)
        arrived = [sent[0]] + [swap(sent[d], "dp", dp, d) for d in (2, 3, 1)]
    else:
        sent = row_rest(part, pre, pre_peer, weight_in, firsts[1], [(part.shape[0], F32)])
        arrived = [lax.psum_scatter(sent[0], "dp", scatter_dimension=0, tiled=True)]
    (grad_weight_in,) = grads(
        [],
        [pre, pre_peer],
        tok_blocks,
        [],
        firsts,
        hidden,
        None,
        [sent[0]],
    )
    input_grad, weight_grad = place(expert_ids, picker, arrived)
    return (input_grad, weight_grad.T, grad_weight_in, grad_weight_out)


def solution(mesh):
    return jax.shard_map(
        functools.partial(per_device, mesh.shape["dp"], mesh.shape["expert"] // 2),
        mesh=mesh,
        in_specs=(
            P(("group", "dp"), "expert"),
            P(("group", "dp"), "expert"),
            P(("group", "dp"), None),
            P(("group", "dp"), None),
            P(None, "dp", "expert"),
            P("dp", "expert"),
        ),
        out_specs=(
            P(("group", "dp"), "expert"),
            P(("group", "dp"), None),
            P("group", "dp", "expert"),
            P(("group", "dp"), "expert"),
        ),
        check_vma=False,
    )
```

```python
import functools

import jax
import jax.numpy as jnp
from jax import lax
from jax.experimental import pallas as pl
from jax.experimental.pallas import tpu as pltpu
from jax.sharding import PartitionSpec as P

F32 = jnp.float32
BF16 = jnp.bfloat16
VMEM = pl.BlockSpec(memory_space=pltpu.VMEM)
SMEM = pl.BlockSpec(memory_space=pltpu.SMEM)
ANY = pl.BlockSpec(memory_space=pl.ANY)
HBM = pl.BlockSpec(memory_space=pltpu.HBM)
LANES = 128
MIB = 2**20

NT = (((1,), (1,)), ((), ()))
TN = (((0,), (0,)), ((), ()))


def params(mib):
    return pltpu.CompilerParams(vmem_limit_bytes=mib * MIB)


def in_hbm(array):
    return pltpu.with_memory_space_constraint(array, pltpu.HBM)


def in_vmem(array):
    return pltpu.with_memory_space_constraint(array, pltpu.VMEM)


STEP = pl.CostEstimate(flops=16 * 10**9, bytes_accessed=1024, transcendentals=0)
FIRST = pl.CostEstimate(flops=18 * 10**9, bytes_accessed=1024, transcendentals=0)


def slot_picker(ids, capacity):
    tok_rows = ids.shape[1]
    routed = jnp.logical_or(ids[0:1] == 0, ids[1:2] == 0)
    row = lax.broadcasted_iota(jnp.int32, (tok_rows, tok_rows), 0)
    col = lax.broadcasted_iota(jnp.int32, (tok_rows, tok_rows), 1)
    before = jnp.where(row < col, 1.0, 0.0).astype(BF16)
    flags = jnp.broadcast_to(jnp.where(routed, 1.0, 0.0), (capacity, tok_rows))
    position = jnp.dot(flags.astype(BF16), before, preferred_element_type=F32)
    slot = lax.broadcasted_iota(jnp.int32, (capacity, tok_rows), 0).astype(F32)
    return jnp.where(position == slot, flags, 0.0).astype(BF16)


def select_kernel(own_ref, other_ref, *refs):
    del own_ref, other_ref
    sources, (in_ref, grad_ref, picker_ref), scratch, sems = refs[:4], refs[4:7], refs[7:11], refs[11]
    copies = [
        pltpu.make_async_copy(a, b, sems.at[i]) for i, (a, b) in enumerate(zip(sources, scratch))
    ]
    for copy in reversed(copies):
        copy.start()
    tok_ref, cot_ref, ids_ref, quant_ref = scratch
    copies[2].wait()
    copies[3].wait()
    capacity, width = in_ref.shape
    ids = ids_ref[...]
    picker = slot_picker(ids, capacity)
    picker_ref[...] = picker
    scaled = quant_ref[...].astype(F32)
    total = scaled[0:1] + scaled[1:2]
    routing = (scaled / total).astype(BF16).astype(F32)
    weight = jnp.where(ids == 0, routing, 0.0)
    rate = jnp.broadcast_to(weight[0:1] + weight[1:2], (LANES, ids.shape[1])).astype(BF16)
    grad_ref[:, width:] = lax.dot_general(picker, rate, NT, preferred_element_type=F32).astype(BF16)
    copies[0].wait()
    in_ref[...] = jnp.dot(picker, tok_ref[...], preferred_element_type=F32).astype(BF16)
    copies[1].wait()
    grad_ref[:, :width] = jnp.dot(picker, cot_ref[...], preferred_element_type=F32).astype(BF16)


def select(firsts, *arrays):
    tok_rows, width = arrays[0].shape
    capacity = tok_rows // 4
    return pl.pallas_call(
        select_kernel,
        in_specs=[SMEM] * 2 + [HBM] * 4,
        out_specs=[VMEM] * 3,
        out_shape=[
            jax.ShapeDtypeStruct((capacity, width), BF16),
            jax.ShapeDtypeStruct((capacity, width + LANES), BF16),
            jax.ShapeDtypeStruct((capacity, tok_rows), BF16),
        ],
        scratch_shapes=[pltpu.VMEM(a.shape, a.dtype) for a in arrays]
        + [pltpu.SemaphoreType.DMA((4,))],
        compiler_params=params(8),
        cost_estimate=FIRST,
        name="select",
    )(*firsts, *(in_hbm(a) for a in arrays))


def project_kernel(nblocks, width, units, first_ref, *refs):
    blocks, w_ref, out_ref = refs[:nblocks], refs[nblocks], refs[-1]
    kinds = w_ref.shape[0]
    half = out_ref.shape[1] // kinds
    rows = jnp.concatenate([b[:, :width] for b in blocks], axis=0)
    start = pl.multiple_of(first_ref[0], half)
    step = min(units, 512)
    at = 0
    for piece in range(0, half, units):
        for kind in range(kinds):
            for j in range(piece, piece + units, step):
                out_ref[:, at : at + step] = lax.dot_general(
                    rows, w_ref[kind, pl.ds(start + j, step), :], NT, preferred_element_type=F32
                ).astype(out_ref.dtype)
                at += step


def project(blocks, weight, first, units, out_type, after):
    kinds, hidden, width = weight.shape
    rows = sum(b.shape[0] for b in blocks)
    return pl.pallas_call(
        functools.partial(project_kernel, len(blocks), width, units),
        in_specs=[SMEM] + [VMEM] * (len(blocks) + 1) + [ANY] * len(after),
        out_specs=VMEM,
        out_shape=jax.ShapeDtypeStruct((rows, kinds * hidden // 2), out_type),
        compiler_params=params(24),
        cost_estimate=STEP,
        name="project",
    )(first, *blocks, in_vmem(weight), *after)


def add_kernel(mine_ref, arrived_ref, *out_refs):
    at = 0
    for out in out_refs:
        cut = slice(at, at + out.shape[1])
        out[...] = (mine_ref[:, cut] + arrived_ref[:, cut].astype(F32)).astype(BF16)
        at = cut.stop


def add(mine, arrived, cuts):
    rows, columns = mine.shape
    return pl.pallas_call(
        add_kernel,
        in_specs=[VMEM] * 2,
        out_specs=[VMEM] * cuts,
        out_shape=[jax.ShapeDtypeStruct((rows, columns // cuts), BF16)] * cuts,
        compiler_params=params(16),
        cost_estimate=STEP,
        name="add",
    )(mine, arrived)


def gate_up(refs, layout, units):
    at = 0
    for nparts, column in layout:
        parts, refs = refs[:nparts], refs[nparts:]
        sums = sum(p[:, column : column + 2 * units].astype(F32) for p in parts)
        yield slice(at, at + sums.shape[0]), sums[:, :units], sums[:, units:]
        at += sums.shape[0]


def hidden_kernel(layout, *refs):
    out_ref = refs[-1]
    for here, gate, up in gate_up(refs, layout, out_ref.shape[1]):
        out_ref[here, :] = (gate * jax.nn.sigmoid(gate) * up).astype(BF16)


def hidden_units(groups, units, after):
    flat = [p for parts, _ in groups for p in parts]
    rows = sum(parts[0].shape[0] for parts, _ in groups)
    return pl.pallas_call(
        functools.partial(hidden_kernel, [(len(parts), column) for parts, column in groups]),
        in_specs=[VMEM] * len(flat) + [ANY] * len(after),
        out_specs=VMEM,
        out_shape=jax.ShapeDtypeStruct((rows, units), BF16),
        compiler_params=params(16),
        cost_estimate=STEP,
        name="hidden",
    )(*flat, *after)


def pre_kernel(layouts, nback, nblocks, width, *refs):
    nsums = sum(n for layout in layouts for n, _ in layout)
    back_parts = refs[nsums : nsums + nback]
    blocks = refs[nsums + nback :][:nblocks]
    out_ref = refs[-1]
    half = back_parts[0].shape[1]
    units = half // len(layouts)
    rates = jnp.concatenate([b[:, width : width + 1].astype(F32) for b in blocks], axis=0)
    routes = {}
    for i, layout in enumerate(layouts):
        first, second = slice(i * units, (i + 1) * units), slice(half + i * units, half + (i + 1) * units)
        for here, gate, up in gate_up(refs, layout, units):
            s = jax.nn.sigmoid(gate)
            back = sum(p[here, first].astype(F32) for p in back_parts)
            hidden = (gate * s * up).astype(BF16).astype(F32)
            route = jnp.sum(hidden * back, axis=1, keepdims=True)
            routes[here.start] = routes[here.start] + route if i else route
            grad = rates[here] * back
            out_ref[here, first] = (grad * up * s * (1.0 + gate * (1.0 - s))).astype(BF16)
            out_ref[here, second] = (grad * gate * s).astype(BF16)
            if i == len(layouts) - 1:
                out_ref[here, 2 * half :] = high_low(routes[here.start])
        refs = refs[sum(n for n, _ in layout) :]


def high_low(value):
    high = value.astype(BF16).astype(F32)
    low = value - high
    lane = lax.broadcasted_iota(jnp.int32, (value.shape[0], LANES), 1)
    return jnp.where(lane == 0, high, jnp.where(lane == 1, low, 0.0)).astype(BF16)


def pre_grads(chunks, back_parts, blocks, width, after):
    half = back_parts[0].shape[1]
    rows = back_parts[0].shape[0]
    flat = [p for groups in chunks for parts, _ in groups for p in parts]
    layouts = [[(len(parts), column) for parts, column in groups] for groups in chunks]
    return pl.pallas_call(
        functools.partial(pre_kernel, layouts, len(back_parts), len(blocks), width),
        in_specs=[VMEM] * (len(flat) + len(back_parts) + len(blocks)) + [ANY] * len(after),
        out_specs=VMEM,
        out_shape=jax.ShapeDtypeStruct((rows, 2 * half + LANES), BF16),
        compiler_params=params(16),
        cost_estimate=STEP,
        name="pre",
    )(*flat, *back_parts, *blocks, *after)


def row_part(pre_ref, w_ref, start):
    half = (pre_ref.shape[1] - LANES) // 2
    return sum(
        jnp.dot(
            pre_ref[:, k * half : (k + 1) * half],
            w_ref[k, pl.ds(start, half), :],
            preferred_element_type=F32,
        )
        for k in range(2)
    )


def row_rest_kernel(first_ref, own_ref, mine_ref, pre_ref, w_ref, *out_refs):
    half = (pre_ref.shape[1] - LANES) // 2
    width = own_ref.shape[1]
    start = pl.multiple_of(first_ref[0], half)
    total = (
        own_ref[...]
        + jnp.dot(pre_ref[:, :half], w_ref[0, pl.ds(start, half), :], preferred_element_type=F32)
        + jnp.dot(
            pre_ref[:, half : 2 * half], w_ref[1, pl.ds(start, half), :], preferred_element_type=F32
        )
    )
    lanes = mine_ref[:, 2 * half :].astype(F32) + pre_ref[:, 2 * half :].astype(F32)
    route = lanes[:, 0:1] + lanes[:, 1:2]
    at = 0
    for out in out_refs:
        rows = out.shape[0]
        out[:, :width] = total[at : at + rows].astype(out.dtype)
        if out.dtype == F32:
            out[:, width:] = jnp.broadcast_to(route[at : at + rows], (rows, LANES)) * jnp.where(
                lax.broadcasted_iota(jnp.int32, (rows, LANES), 1) == 0, 1.0, 0.0
            )
        else:
            out[:, width:] = high_low(route[at : at + rows])
        at += rows


def row_rest(own, mine, pre, weight, first, outs):
    rows, width = own.shape
    return pl.pallas_call(
        row_rest_kernel,
        in_specs=[SMEM] + [VMEM] * 4,
        out_specs=[VMEM] * len(outs),
        out_shape=[jax.ShapeDtypeStruct((n, width + LANES), kind) for n, kind in outs],
        compiler_params=params(24),
        cost_estimate=STEP,
        name="row_rest",
    )(first, own, mine, pre, in_vmem(weight))


def grads_kernel(outs, nin, ntok, ncot, nrows, nafter, nbefore, own_ref, other_ref, *refs):
    out_sources, refs = refs[: len(outs)], refs[len(outs) :]
    in_sources, refs = refs[:nin], refs[nin:]
    toks, refs = refs[:ntok], refs[ntok:]
    cots, refs = refs[:ncot], refs[ncot:]
    summed, refs = refs[:nrows], refs[nrows:]
    refs = refs[nafter + nbefore :]
    out_ref, *extra, rows_of, buf, sem = refs
    hidden, width = out_ref.shape[-2:]
    half = hidden // 2
    ring, step = buf.shape[:2]
    at = 0
    for t in toks:
        rows_of[at : at + t.shape[0], :] = t[...]
        at += t.shape[0]
    for c in cots:
        rows_of[at : at + c.shape[0], :] = (
            c[:, width : width + 1].astype(F32) * c[:, :width].astype(F32)
        ).astype(BF16)
        at += c.shape[0]
    starts = [pl.multiple_of(ref[0], half) for ref in (own_ref, other_ref)]
    tiles = []
    for source, (side, first, end) in zip(out_sources, outs):
        for j in range(first, end, step):
            tiles.append((source, j, out_ref.at[pl.ds(starts[side] + j, step)]))
    for side, source in enumerate(in_sources):
        for kind in range(2):
            for j in range(0, half, step):
                target = out_ref.at[kind, pl.ds(starts[side] + j, step)]
                tiles.append((source, kind * half + j, target))
    copies = []
    for i, (source, column, target) in enumerate(tiles):
        if i >= ring:
            copies[i - ring].wait()
        buf[i % ring] = lax.dot_general(
            source[:, column : column + step], rows_of[...], TN, preferred_element_type=F32
        )
        copies.append(pltpu.make_async_copy(buf.at[i % ring], target, sem.at[i % ring]))
        copies[-1].start()
    for more in extra:
        more[...] = row_part(*summed, starts[0]) if summed else jnp.zeros_like(more)
    for copy in copies[max(0, len(copies) - ring) :]:
        copy.wait()


def grads(outs, ins, tok_blocks, cot_blocks, firsts, hidden, so_far, after=(), extra=None):
    width = tok_blocks[0].shape[1] if ins else cot_blocks[0].shape[1] - LANES
    sources = [piece[0] for piece in outs]
    places = [piece[1:] for piece in outs]
    rows = (sources + list(ins))[0].shape[0]
    step = min(hidden // 2, 256)
    ring = min(8, (sum(end - first for _, first, end in places) + len(ins) * hidden) // step)
    before = [] if so_far is None else [in_hbm(so_far)]
    toks = tok_blocks if ins else []
    shape = (2, hidden, width) if ins else (hidden, width)
    out_shape = [pltpu.HBM(shape, F32)]
    summed = []
    if extra == ():
        out_shape.append(jax.ShapeDtypeStruct((8, LANES), F32))
    elif extra:
        out_shape.append(jax.ShapeDtypeStruct((rows, width), F32))
        summed = [extra[0], in_vmem(extra[1])]
    operands = [*sources, *ins, *toks, *cot_blocks, *summed]
    sizes = (len(ins), len(toks), len(cot_blocks), len(summed), len(after), len(before))
    return pl.pallas_call(
        functools.partial(grads_kernel, places, *sizes),
        in_specs=[SMEM] * 2 + [VMEM] * len(operands) + [ANY] * len(after) + [HBM] * len(before),
        out_specs=[HBM] + [VMEM] * (len(out_shape) - 1),
        out_shape=out_shape,
        scratch_shapes=[
            pltpu.VMEM((rows, width), BF16),
            pltpu.VMEM((ring, step, width), F32),
            pltpu.SemaphoreType.DMA((ring,)),
        ],
        input_output_aliases=(
            {2 + len(operands) + len(after): 0} if before else {}
        ),
        compiler_params=params(28),
        cost_estimate=STEP,
        name="grads",
    )(*firsts, *operands, *after, *before)


def place_kernel(ids_ref, picker_ref, *refs):
    blocks, (in_ref, weight_ref) = refs[:-2], refs[-2:]
    width = in_ref.shape[1]
    capacity = picker_ref.shape[0]
    picker = picker_ref[...]
    total = sum(b[:, :width].astype(F32) for b in blocks)
    lanes = sum(b[:, width:].astype(F32) for b in blocks)
    in_ref[...] = lax.dot_general(
        picker, total.astype(BF16), TN, preferred_element_type=F32
    ).astype(BF16)
    route = jnp.broadcast_to(lanes[:, 0:1] + lanes[:, 1:2], (capacity, LANES))
    high = route.astype(BF16)
    low = (route - high.astype(F32)).astype(BF16)
    spread = lax.dot_general(high, picker, TN, preferred_element_type=F32) + lax.dot_general(
        low, picker, TN, preferred_element_type=F32
    )
    ids = ids_ref[...]
    weight_ref[...] = jnp.where(ids == 0, spread[: ids.shape[0]], 0.0).astype(BF16)


def place(expert_ids, picker, blocks):
    width = blocks[0].shape[1] - LANES
    return pl.pallas_call(
        place_kernel,
        in_specs=[VMEM] * (2 + len(blocks)),
        out_specs=[VMEM] * 2,
        out_shape=[
            jax.ShapeDtypeStruct((picker.shape[1], width), BF16),
            jax.ShapeDtypeStruct(expert_ids.shape, BF16),
        ],
        compiler_params=params(8),
        cost_estimate=STEP,
        name="place",
    )(expert_ids, picker, *blocks)


def swap(array, axis, size, distance):
    return lax.ppermute(array, axis, [(i, i ^ distance) for i in range(size)])


def relay_kernel(nblocks, *refs):
    blocks, out_ref = refs[:nblocks], refs[-1]
    at = 0
    for b in blocks:
        out_ref[at : at + b.shape[0], :] = b[...]
        at += b.shape[0]


def relay(blocks, after):
    rows = sum(b.shape[0] for b in blocks)
    return pl.pallas_call(
        functools.partial(relay_kernel, len(blocks)),
        in_specs=[VMEM] * len(blocks) + [ANY],
        out_specs=VMEM,
        out_shape=jax.ShapeDtypeStruct((rows, blocks[0].shape[1]), blocks[0].dtype),
        compiler_params=params(8),
        cost_estimate=STEP,
        name="relay",
    )(*blocks, after)


def per_device(dp, chips, tokens, cotangent, expert_ids, quantized, weight_in, weight_out):
    experts = 2 * chips
    width = tokens.shape[1]
    hidden = weight_in.shape[1]
    half = hidden // 2
    core = lax.rem(lax.axis_index("expert"), 2)
    firsts = [(c * half).astype(jnp.int32).reshape(1) for c in (core, 1 - core)]
    direct = dp == 4

    expert_ids, quantized = expert_ids.T, quantized.T
    weight_out = weight_out.reshape((1,) + weight_out.shape)
    send_in, send_grad, picker = select(firsts, tokens, cotangent, expert_ids, quantized)
    if direct:
        tok_blocks = [send_in] + [swap(send_in, "dp", dp, d) for d in range(1, dp)]
        cot_blocks = [send_grad, swap(send_grad, "dp", dp, 2)]
        groups = [tok_blocks[:2], tok_blocks[2:]]
    else:
        tok_blocks = [lax.all_gather(send_in, "dp", axis=0, tiled=True)]
        cot_blocks = [lax.all_gather(send_grad, "dp", axis=0, tiled=True)]
        groups = [tok_blocks]

    pieces, units = 1, half

    def chip_sums(blocks, weight, last, cuts=1, meanwhile=None):
        theirs = project(blocks, weight, firsts[1], units, BF16, [last])
        arrived = swap(theirs, "expert", experts, 1)
        last = meanwhile(theirs) if meanwhile is not None else theirs
        mine = project(blocks, weight, firsts[0], units, F32, [last])
        return add(mine, arrived, cuts)

    def all_chips(chip):
        return [chip] + [swap(chip, "expert", experts, 2 * k) for k in range(1, chips)]

    def pass_on(after):
        block = relay([send_grad], after)
        cot_blocks.insert(1, swap(block, "dp", dp, 1))
        cot_blocks.append(swap(block, "dp", dp, 3))
        return block

    chunks, last = [[] for _ in range(pieces)], send_grad
    for blocks in groups[:-1]:
        (last,) = chip_sums(blocks, weight_in, last)
        parts = all_chips(last)
        for i, groups_of in enumerate(chunks):
            groups_of.append((parts, i * 2 * units))
    if direct:
        last = pass_on(last)
    cuts = chip_sums(groups[-1], weight_in, last, pieces)
    for groups_of, cut in zip(chunks, cuts):
        groups_of.append((all_chips(cut), 0))
    back = all_chips(*chip_sums(cot_blocks, weight_out, cuts[-1]))

    mine = hidden_units(chunks[0], units, [back[0]])
    peer = swap(mine, "expert", experts, 1)
    middle = half // 2 if half % 512 == 0 else 0
    grad_weight_out, *mark = grads(
        [(mine, 0, 0, half)],
        [],
        [],
        cot_blocks,
        firsts,
        hidden,
        None,
        extra=None if middle else (),
    )
    if middle:
        grad_weight_out, *mark = grads(
            [(peer, 1, 0, middle)], [], [], cot_blocks, firsts, hidden, grad_weight_out, extra=()
        )
    pre = pre_grads(chunks, back, cot_blocks, width, mark)
    pre_peer = swap(pre, "expert", experts, 1)
    grad_weight_out, part = grads(
        [(peer, 1, middle, half)],
        [],
        [],
        cot_blocks,
        firsts,
        hidden,
        grad_weight_out,
        extra=(pre, weight_in),
    )
    if direct:
        cap = send_in.shape[0]
        outs = [(cap, F32)] + [(cap, BF16)] * (dp - 1)
        sent = row_rest(part, pre, pre_peer, weight_in, firsts[1], outs)
        arrived = [sent[0]] + [swap(sent[d], "dp", dp, d) for d in (2, 3, 1)]
    else:
        sent = row_rest(part, pre, pre_peer, weight_in, firsts[1], [(part.shape[0], F32)])
        arrived = [lax.psum_scatter(sent[0], "dp", scatter_dimension=0, tiled=True)]
    (grad_weight_in,) = grads(
        [],
        [pre, pre_peer],
        tok_blocks,
        [],
        firsts,
        hidden,
        None,
        [sent[0]],
    )
    input_grad, weight_grad = place(expert_ids, picker, arrived)
    return (input_grad, weight_grad.T, grad_weight_in, grad_weight_out)


def solution(mesh):
    return jax.shard_map(
        functools.partial(per_device, mesh.shape["dp"], mesh.shape["expert"] // 2),
        mesh=mesh,
        in_specs=(
            P(("group", "dp"), "expert"),
            P(("group", "dp"), "expert"),
            P(("group", "dp"), None),
            P(("group", "dp"), None),
            P(None, "dp", "expert"),
            P("dp", "expert"),
        ),
        out_specs=(
            P(("group", "dp"), "expert"),
            P(("group", "dp"), None),
            P("group", "dp", "expert"),
            P(("group", "dp"), "expert"),
        ),
        check_vma=False,
    )
```

```python
import functools

import jax
import jax.numpy as jnp
from jax import lax
from jax.experimental import pallas as pl
from jax.experimental.pallas import tpu as pltpu
from jax.sharding import PartitionSpec as P

F32 = jnp.float32
BF16 = jnp.bfloat16
VMEM = pl.BlockSpec(memory_space=pltpu.VMEM)
SMEM = pl.BlockSpec(memory_space=pltpu.SMEM)
ANY = pl.BlockSpec(memory_space=pl.ANY)
HBM = pl.BlockSpec(memory_space=pltpu.HBM)
LANES = 128
MIB = 2**20

NT = (((1,), (1,)), ((), ()))
TN = (((0,), (0,)), ((), ()))


def params(mib):
    return pltpu.CompilerParams(vmem_limit_bytes=mib * MIB)


def in_hbm(array):
    return pltpu.with_memory_space_constraint(array, pltpu.HBM)


def in_vmem(array):
    return pltpu.with_memory_space_constraint(array, pltpu.VMEM)


STEP = pl.CostEstimate(flops=16 * 10**9, bytes_accessed=1024, transcendentals=0)
FIRST = pl.CostEstimate(flops=18 * 10**9, bytes_accessed=1024, transcendentals=0)


def slot_picker(ids, capacity):
    tok_rows = ids.shape[1]
    routed = jnp.logical_or(ids[0:1] == 0, ids[1:2] == 0)
    row = lax.broadcasted_iota(jnp.int32, (tok_rows, tok_rows), 0)
    col = lax.broadcasted_iota(jnp.int32, (tok_rows, tok_rows), 1)
    before = jnp.where(row < col, 1.0, 0.0).astype(BF16)
    flags = jnp.broadcast_to(jnp.where(routed, 1.0, 0.0), (capacity, tok_rows))
    position = jnp.dot(flags.astype(BF16), before, preferred_element_type=F32)
    slot = lax.broadcasted_iota(jnp.int32, (capacity, tok_rows), 0).astype(F32)
    return jnp.where(position == slot, flags, 0.0).astype(BF16)


def select_kernel(own_ref, other_ref, *refs):
    del own_ref, other_ref
    sources, (in_ref, grad_ref, picker_ref), scratch, sems = refs[:4], refs[4:7], refs[7:11], refs[11]
    copies = [
        pltpu.make_async_copy(a, b, sems.at[i]) for i, (a, b) in enumerate(zip(sources, scratch))
    ]
    for copy in reversed(copies):
        copy.start()
    tok_ref, cot_ref, ids_ref, quant_ref = scratch
    copies[2].wait()
    copies[3].wait()
    capacity, width = in_ref.shape
    ids = ids_ref[...]
    picker = slot_picker(ids, capacity)
    picker_ref[...] = picker
    scaled = quant_ref[...].astype(F32)
    total = scaled[0:1] + scaled[1:2]
    routing = (scaled / total).astype(BF16).astype(F32)
    weight = jnp.where(ids == 0, routing, 0.0)
    rate = jnp.broadcast_to(weight[0:1] + weight[1:2], (LANES, ids.shape[1])).astype(BF16)
    grad_ref[:, width:] = lax.dot_general(picker, rate, NT, preferred_element_type=F32).astype(BF16)
    copies[0].wait()
    in_ref[...] = jnp.dot(picker, tok_ref[...], preferred_element_type=F32).astype(BF16)
    copies[1].wait()
    grad_ref[:, :width] = jnp.dot(picker, cot_ref[...], preferred_element_type=F32).astype(BF16)


def select(firsts, *arrays):
    tok_rows, width = arrays[0].shape
    capacity = tok_rows // 4
    return pl.pallas_call(
        select_kernel,
        in_specs=[SMEM] * 2 + [HBM] * 4,
        out_specs=[VMEM] * 3,
        out_shape=[
            jax.ShapeDtypeStruct((capacity, width), BF16),
            jax.ShapeDtypeStruct((capacity, width + LANES), BF16),
            jax.ShapeDtypeStruct((capacity, tok_rows), BF16),
        ],
        scratch_shapes=[pltpu.VMEM(a.shape, a.dtype) for a in arrays]
        + [pltpu.SemaphoreType.DMA((4,))],
        compiler_params=params(8),
        cost_estimate=FIRST,
        name="select",
    )(*firsts, *(in_hbm(a) for a in arrays))


def project_kernel(nblocks, width, units, first_ref, *refs):
    blocks, w_ref, out_ref = refs[:nblocks], refs[nblocks], refs[-1]
    kinds = w_ref.shape[0]
    half = out_ref.shape[1] // kinds
    rows = jnp.concatenate([b[:, :width] for b in blocks], axis=0)
    start = pl.multiple_of(first_ref[0], half)
    step = min(units, 512)
    at = 0
    for piece in range(0, half, units):
        for kind in range(kinds):
            for j in range(piece, piece + units, step):
                out_ref[:, at : at + step] = lax.dot_general(
                    rows, w_ref[kind, pl.ds(start + j, step), :], NT, preferred_element_type=F32
                ).astype(out_ref.dtype)
                at += step


def project(blocks, weight, first, units, out_type, after):
    kinds, hidden, width = weight.shape
    rows = sum(b.shape[0] for b in blocks)
    return pl.pallas_call(
        functools.partial(project_kernel, len(blocks), width, units),
        in_specs=[SMEM] + [VMEM] * (len(blocks) + 1) + [ANY] * len(after),
        out_specs=VMEM,
        out_shape=jax.ShapeDtypeStruct((rows, kinds * hidden // 2), out_type),
        compiler_params=params(24),
        cost_estimate=STEP,
        name="project",
    )(first, *blocks, in_vmem(weight), *after)


def add_kernel(mine_ref, arrived_ref, *out_refs):
    at = 0
    for out in out_refs:
        cut = slice(at, at + out.shape[1])
        out[...] = (mine_ref[:, cut] + arrived_ref[:, cut].astype(F32)).astype(BF16)
        at = cut.stop


def add(mine, arrived, cuts):
    rows, columns = mine.shape
    return pl.pallas_call(
        add_kernel,
        in_specs=[VMEM] * 2,
        out_specs=[VMEM] * cuts,
        out_shape=[jax.ShapeDtypeStruct((rows, columns // cuts), BF16)] * cuts,
        compiler_params=params(16),
        cost_estimate=STEP,
        name="add",
    )(mine, arrived)


def gate_up(refs, layout, units):
    at = 0
    for nparts, column in layout:
        parts, refs = refs[:nparts], refs[nparts:]
        sums = sum(p[:, column : column + 2 * units].astype(F32) for p in parts)
        yield slice(at, at + sums.shape[0]), sums[:, :units], sums[:, units:]
        at += sums.shape[0]


def hidden_kernel(layout, *refs):
    out_ref = refs[-1]
    for here, gate, up in gate_up(refs, layout, out_ref.shape[1]):
        out_ref[here, :] = (gate * jax.nn.sigmoid(gate) * up).astype(BF16)


def hidden_units(groups, units, after):
    flat = [p for parts, _ in groups for p in parts]
    rows = sum(parts[0].shape[0] for parts, _ in groups)
    return pl.pallas_call(
        functools.partial(hidden_kernel, [(len(parts), column) for parts, column in groups]),
        in_specs=[VMEM] * len(flat) + [ANY] * len(after),
        out_specs=VMEM,
        out_shape=jax.ShapeDtypeStruct((rows, units), BF16),
        compiler_params=params(16),
        cost_estimate=STEP,
        name="hidden",
    )(*flat, *after)


def pre_kernel(layouts, nback, nblocks, width, *refs):
    nsums = sum(n for layout in layouts for n, _ in layout)
    back_parts = refs[nsums : nsums + nback]
    blocks = refs[nsums + nback :][:nblocks]
    out_ref = refs[-1]
    half = back_parts[0].shape[1]
    units = half // len(layouts)
    rates = jnp.concatenate([b[:, width : width + 1].astype(F32) for b in blocks], axis=0)
    routes = {}
    for i, layout in enumerate(layouts):
        first, second = slice(i * units, (i + 1) * units), slice(half + i * units, half + (i + 1) * units)
        for here, gate, up in gate_up(refs, layout, units):
            s = jax.nn.sigmoid(gate)
            back = sum(p[here, first].astype(F32) for p in back_parts)
            hidden = (gate * s * up).astype(BF16).astype(F32)
            route = jnp.sum(hidden * back, axis=1, keepdims=True)
            routes[here.start] = routes[here.start] + route if i else route
            grad = rates[here] * back
            out_ref[here, first] = (grad * up * s * (1.0 + gate * (1.0 - s))).astype(BF16)
            out_ref[here, second] = (grad * gate * s).astype(BF16)
            if i == len(layouts) - 1:
                out_ref[here, 2 * half :] = high_low(routes[here.start])
        refs = refs[sum(n for n, _ in layout) :]


def high_low(value):
    high = value.astype(BF16).astype(F32)
    low = value - high
    lane = lax.broadcasted_iota(jnp.int32, (value.shape[0], LANES), 1)
    return jnp.where(lane == 0, high, jnp.where(lane == 1, low, 0.0)).astype(BF16)


def pre_grads(chunks, back_parts, blocks, width, after):
    half = back_parts[0].shape[1]
    rows = back_parts[0].shape[0]
    flat = [p for groups in chunks for parts, _ in groups for p in parts]
    layouts = [[(len(parts), column) for parts, column in groups] for groups in chunks]
    return pl.pallas_call(
        functools.partial(pre_kernel, layouts, len(back_parts), len(blocks), width),
        in_specs=[VMEM] * (len(flat) + len(back_parts) + len(blocks)) + [ANY] * len(after),
        out_specs=VMEM,
        out_shape=jax.ShapeDtypeStruct((rows, 2 * half + LANES), BF16),
        compiler_params=params(16),
        cost_estimate=STEP,
        name="pre",
    )(*flat, *back_parts, *blocks, *after)


def row_part(pre_ref, w_ref, start):
    half = (pre_ref.shape[1] - LANES) // 2
    return sum(
        jnp.dot(
            pre_ref[:, k * half : (k + 1) * half],
            w_ref[k, pl.ds(start, half), :],
            preferred_element_type=F32,
        )
        for k in range(2)
    )


def row_rest_kernel(first_ref, own_ref, mine_ref, pre_ref, w_ref, *out_refs):
    half = (pre_ref.shape[1] - LANES) // 2
    width = own_ref.shape[1]
    start = pl.multiple_of(first_ref[0], half)
    total = (
        own_ref[...]
        + jnp.dot(pre_ref[:, :half], w_ref[0, pl.ds(start, half), :], preferred_element_type=F32)
        + jnp.dot(
            pre_ref[:, half : 2 * half], w_ref[1, pl.ds(start, half), :], preferred_element_type=F32
        )
    )
    lanes = mine_ref[:, 2 * half :].astype(F32) + pre_ref[:, 2 * half :].astype(F32)
    route = lanes[:, 0:1] + lanes[:, 1:2]
    at = 0
    for out in out_refs:
        rows = out.shape[0]
        out[:, :width] = total[at : at + rows].astype(out.dtype)
        if out.dtype == F32:
            out[:, width:] = jnp.broadcast_to(route[at : at + rows], (rows, LANES)) * jnp.where(
                lax.broadcasted_iota(jnp.int32, (rows, LANES), 1) == 0, 1.0, 0.0
            )
        else:
            out[:, width:] = high_low(route[at : at + rows])
        at += rows


def row_rest(own, mine, pre, weight, first, outs):
    rows, width = own.shape
    return pl.pallas_call(
        row_rest_kernel,
        in_specs=[SMEM] + [VMEM] * 4,
        out_specs=[VMEM] * len(outs),
        out_shape=[jax.ShapeDtypeStruct((n, width + LANES), kind) for n, kind in outs],
        compiler_params=params(24),
        cost_estimate=STEP,
        name="row_rest",
    )(first, own, mine, pre, in_vmem(weight))


def grads_kernel(outs, nin, ntok, ncot, nrows, nafter, nbefore, own_ref, other_ref, *refs):
    out_sources, refs = refs[: len(outs)], refs[len(outs) :]
    in_sources, refs = refs[:nin], refs[nin:]
    toks, refs = refs[:ntok], refs[ntok:]
    cots, refs = refs[:ncot], refs[ncot:]
    summed, refs = refs[:nrows], refs[nrows:]
    refs = refs[nafter + nbefore :]
    out_ref, *extra, rows_of, buf, sem = refs
    hidden, width = out_ref.shape[-2:]
    half = hidden // 2
    ring, step = buf.shape[:2]
    at = 0
    for t in toks:
        rows_of[at : at + t.shape[0], :] = t[...]
        at += t.shape[0]
    for c in cots:
        rows_of[at : at + c.shape[0], :] = (
            c[:, width : width + 1].astype(F32) * c[:, :width].astype(F32)
        ).astype(BF16)
        at += c.shape[0]
    starts = [pl.multiple_of(ref[0], half) for ref in (own_ref, other_ref)]
    tiles = []
    for source, (side, first, end) in zip(out_sources, outs):
        for j in range(first, end, step):
            tiles.append((source, j, out_ref.at[pl.ds(starts[side] + j, step)]))
    for side, source in enumerate(in_sources):
        for kind in range(2):
            for j in range(0, half, step):
                target = out_ref.at[kind, pl.ds(starts[side] + j, step)]
                tiles.append((source, kind * half + j, target))
    copies = []
    for i, (source, column, target) in enumerate(tiles):
        if i >= ring:
            copies[i - ring].wait()
        buf[i % ring] = lax.dot_general(
            source[:, column : column + step], rows_of[...], TN, preferred_element_type=F32
        )
        copies.append(pltpu.make_async_copy(buf.at[i % ring], target, sem.at[i % ring]))
        copies[-1].start()
    for more in extra:
        more[...] = row_part(*summed, starts[0]) if summed else jnp.zeros_like(more)
    for copy in copies[max(0, len(copies) - ring) :]:
        copy.wait()


def grads(outs, ins, tok_blocks, cot_blocks, firsts, hidden, so_far, after=(), extra=None):
    width = tok_blocks[0].shape[1] if ins else cot_blocks[0].shape[1] - LANES
    sources = [piece[0] for piece in outs]
    places = [piece[1:] for piece in outs]
    rows = (sources + list(ins))[0].shape[0]
    step = min(hidden // 2, 256)
    ring = min(8, (sum(end - first for _, first, end in places) + len(ins) * hidden) // step)
    before = [] if so_far is None else [in_hbm(so_far)]
    toks = tok_blocks if ins else []
    shape = (2, hidden, width) if ins else (hidden, width)
    out_shape = [pltpu.HBM(shape, F32)]
    summed = []
    if extra == ():
        out_shape.append(jax.ShapeDtypeStruct((8, LANES), F32))
    elif extra:
        out_shape.append(jax.ShapeDtypeStruct((rows, width), F32))
        summed = [extra[0], in_vmem(extra[1])]
    operands = [*sources, *ins, *toks, *cot_blocks, *summed]
    sizes = (len(ins), len(toks), len(cot_blocks), len(summed), len(after), len(before))
    return pl.pallas_call(
        functools.partial(grads_kernel, places, *sizes),
        in_specs=[SMEM] * 2 + [VMEM] * len(operands) + [ANY] * len(after) + [HBM] * len(before),
        out_specs=[HBM] + [VMEM] * (len(out_shape) - 1),
        out_shape=out_shape,
        scratch_shapes=[
            pltpu.VMEM((rows, width), BF16),
            pltpu.VMEM((ring, step, width), F32),
            pltpu.SemaphoreType.DMA((ring,)),
        ],
        input_output_aliases=(
            {2 + len(operands) + len(after): 0} if before else {}
        ),
        compiler_params=params(28),
        cost_estimate=STEP,
        name="grads",
    )(*firsts, *operands, *after, *before)


def place_kernel(ids_ref, picker_ref, *refs):
    blocks, (in_ref, weight_ref) = refs[:-2], refs[-2:]
    width = in_ref.shape[1]
    capacity = picker_ref.shape[0]
    picker = picker_ref[...]
    total = sum(b[:, :width].astype(F32) for b in blocks)
    lanes = sum(b[:, width:].astype(F32) for b in blocks)
    in_ref[...] = lax.dot_general(
        picker, total.astype(BF16), TN, preferred_element_type=F32
    ).astype(BF16)
    route = jnp.broadcast_to(lanes[:, 0:1] + lanes[:, 1:2], (capacity, LANES))
    high = route.astype(BF16)
    low = (route - high.astype(F32)).astype(BF16)
    spread = lax.dot_general(high, picker, TN, preferred_element_type=F32) + lax.dot_general(
        low, picker, TN, preferred_element_type=F32
    )
    ids = ids_ref[...]
    weight_ref[...] = jnp.where(ids == 0, spread[: ids.shape[0]], 0.0).astype(BF16)


def place(expert_ids, picker, blocks):
    width = blocks[0].shape[1] - LANES
    return pl.pallas_call(
        place_kernel,
        in_specs=[VMEM] * (2 + len(blocks)),
        out_specs=[VMEM] * 2,
        out_shape=[
            jax.ShapeDtypeStruct((picker.shape[1], width), BF16),
            jax.ShapeDtypeStruct(expert_ids.shape, BF16),
        ],
        compiler_params=params(8),
        cost_estimate=STEP,
        name="place",
    )(expert_ids, picker, *blocks)


def swap(array, axis, size, distance):
    return lax.ppermute(array, axis, [(i, i ^ distance) for i in range(size)])


def relay_kernel(nblocks, *refs):
    blocks, out_ref = refs[:nblocks], refs[-1]
    at = 0
    for b in blocks:
        out_ref[at : at + b.shape[0], :] = b[...]
        at += b.shape[0]


def relay(blocks, after):
    rows = sum(b.shape[0] for b in blocks)
    return pl.pallas_call(
        functools.partial(relay_kernel, len(blocks)),
        in_specs=[VMEM] * len(blocks) + [ANY],
        out_specs=VMEM,
        out_shape=jax.ShapeDtypeStruct((rows, blocks[0].shape[1]), blocks[0].dtype),
        compiler_params=params(8),
        cost_estimate=STEP,
        name="relay",
    )(*blocks, after)


def per_device(dp, chips, tokens, cotangent, expert_ids, quantized, weight_in, weight_out):
    experts = 2 * chips
    width = tokens.shape[1]
    hidden = weight_in.shape[1]
    half = hidden // 2
    core = lax.rem(lax.axis_index("expert"), 2)
    firsts = [(c * half).astype(jnp.int32).reshape(1) for c in (core, 1 - core)]
    direct = dp == 4

    expert_ids, quantized = expert_ids.T, quantized.T
    weight_out = weight_out.reshape((1,) + weight_out.shape)
    send_in, send_grad, picker = select(firsts, tokens, cotangent, expert_ids, quantized)
    if direct:
        tok_blocks = [send_in] + [swap(send_in, "dp", dp, d) for d in range(1, dp)]
        cot_blocks = [send_grad, swap(send_grad, "dp", dp, 2)]
        groups = [tok_blocks[:2], tok_blocks[2:]]
    else:
        tok_blocks = [lax.all_gather(send_in, "dp", axis=0, tiled=True)]
        cot_blocks = [lax.all_gather(send_grad, "dp", axis=0, tiled=True)]
        groups = [tok_blocks]

    pieces, units = 1, half

    def chip_sums(blocks, weight, last, cuts=1, meanwhile=None):
        theirs = project(blocks, weight, firsts[1], units, BF16, [last])
        arrived = swap(theirs, "expert", experts, 1)
        last = meanwhile(theirs) if meanwhile is not None else theirs
        mine = project(blocks, weight, firsts[0], units, F32, [last])
        return add(mine, arrived, cuts)

    def all_chips(chip):
        return [chip] + [swap(chip, "expert", experts, 2 * k) for k in range(1, chips)]

    def pass_on(after):
        block = relay([send_grad], after)
        cot_blocks.append(swap(block, "dp", dp, 3))
        cot_blocks.insert(1, swap(block, "dp", dp, 1))
        return block

    chunks, last = [[] for _ in range(pieces)], send_grad
    for blocks in groups[:-1]:
        (last,) = chip_sums(blocks, weight_in, last)
        parts = all_chips(last)
        for i, groups_of in enumerate(chunks):
            groups_of.append((parts, i * 2 * units))
    if direct:
        last = pass_on(last)
    cuts = chip_sums(groups[-1], weight_in, last, pieces)
    for groups_of, cut in zip(chunks, cuts):
        groups_of.append((all_chips(cut), 0))
    back = all_chips(*chip_sums(cot_blocks, weight_out, cuts[-1]))

    mine = hidden_units(chunks[0], units, [back[0]])
    peer = swap(mine, "expert", experts, 1)
    middle = half // 2 if half % 512 == 0 else 0
    grad_weight_out, *mark = grads(
        [(mine, 0, 0, half)],
        [],
        [],
        cot_blocks,
        firsts,
        hidden,
        None,
        extra=None if middle else (),
    )
    if middle:
        grad_weight_out, *mark = grads(
            [(peer, 1, 0, middle)], [], [], cot_blocks, firsts, hidden, grad_weight_out, extra=()
        )
    pre = pre_grads(chunks, back, cot_blocks, width, mark)
    pre_peer = swap(pre, "expert", experts, 1)
    grad_weight_out, part = grads(
        [(peer, 1, middle, half)],
        [],
        [],
        cot_blocks,
        firsts,
        hidden,
        grad_weight_out,
        extra=(pre, weight_in),
    )
    if direct:
        cap = send_in.shape[0]
        outs = [(cap, F32)] + [(cap, BF16)] * (dp - 1)
        sent = row_rest(part, pre, pre_peer, weight_in, firsts[1], outs)
        arrived = [sent[0]] + [swap(sent[d], "dp", dp, d) for d in (2, 3, 1)]
    else:
        sent = row_rest(part, pre, pre_peer, weight_in, firsts[1], [(part.shape[0], F32)])
        arrived = [lax.psum_scatter(sent[0], "dp", scatter_dimension=0, tiled=True)]
    (grad_weight_in,) = grads(
        [],
        [pre, pre_peer],
        tok_blocks,
        [],
        firsts,
        hidden,
        None,
        [sent[0]],
    )
    input_grad, weight_grad = place(expert_ids, picker, arrived)
    return (input_grad, weight_grad.T, grad_weight_in, grad_weight_out)


def solution(mesh):
    return jax.shard_map(
        functools.partial(per_device, mesh.shape["dp"], mesh.shape["expert"] // 2),
        mesh=mesh,
        in_specs=(
            P(("group", "dp"), "expert"),
            P(("group", "dp"), "expert"),
            P(("group", "dp"), None),
            P(("group", "dp"), None),
            P(None, "dp", "expert"),
            P("dp", "expert"),
        ),
        out_specs=(
            P(("group", "dp"), "expert"),
            P(("group", "dp"), None),
            P("group", "dp", "expert"),
            P(("group", "dp"), "expert"),
        ),
        check_vma=False,
    )
```
